128 devices in a mesh: gx: 16 (over z, y), gy: 8 (over x, core).
Axes of the slice: x: 4, y: 4, z: 4, core: 2. Of those that a mesh axis runs over, the one named last changes fastest.
Arguments:
- user_table: float32 [524288, 128], P(('gx', 'gy'))
- item_table: float32 [524288, 128], P(('gx', 'gy'))
- item_owner: int32 [786432, 1], P(('gx', 'gy')), may hold values from 0 to 127; in each aligned block of 6144 rows (0 to 6143, 6144 to 12287, ...) at most 60 rows name the same one
- item_row: int32 [786432], P(('gx', 'gy')), may hold values from 0 to 4095
- user_confidence: float32 [786432], P(('gx', 'gy')), may hold values from 0.5 to 8
- user_rating: float32 [786432], P(('gx', 'gy')), may hold values from -12 to 12
- user_counts: int32 [6144, 4], P(('gx', 'gy')), may hold values from 1 to 64, 112 in all within a row
- user_owner: int32 [786432, 1], P(('gx', 'gy')), may hold values from 0 to 127; in each aligned block of 6144 rows (0 to 6143, 6144 to 12287, ...) at most 60 rows name the same one
- user_row: int32 [786432], P(('gx', 'gy')), may hold values from 0 to 4095
- item_confidence: float32 [786432], P(('gx', 'gy')), may hold values from 0.5 to 8
- item_rating: float32 [786432], P(('gx', 'gy')), may hold values from -12 to 12
- item_counts: int32 [6144, 4], P(('gx', 'gy')), may hold values from 1 to 64, 112 in all within a row
Outputs:
- new_users: float32 [524288, 128], P(('gx', 'gy'))
- new_items: float32 [524288, 128], P(('gx', 'gy'))
The draws below stay inside these ranges and needn't reach their ends.
Inputs may be any that keep to these rules, and one draw needn't show every extreme that they name: `item_owner`: among the 6144 slots of one device at most 60 name the same owner, a bound that some block reaches. `user_owner`: among the 6144 slots of one device at most 60 name the same owner, a bound that some block reaches. `user_counts`: each row of 4 counts sums to 112. `item_counts`: each row of 4 counts sums to 112.
All inputs are finite; a program needn't handle non-finite values.
Results may differ from the reference program's by a relative error of at most 0.024.
The reference program's roundings to bfloat16 on the way count: a program that leaves them out, or rounds other values in their place, can miss the bound.
Values may be sent and summed in bfloat16 or wider, within the bound.
No kernel may reach another device: no remote copies, remote signals or barrier semaphores. Data moves between devices by JAX's collectives and lax.ppermute only.
A program may use at most 128 MiB of HBM per device.

```python
import math
import jax
import jax.numpy as jnp
import numpy as np
from jax import lax

K = 128
UB = 4
BLOCK_ROWS = 128
LIVE = 112
SEG_MAX = 64
ITERS = 8
BLOCKS = 48
TAB_DEV = 4096
BATCH_DEV = 192
NNZ_DEV = 6144
CAP = 60
NNZ_ALL = 786432
BLOCKS_ALL = 6144
N_GX = 16
N_GY = 8
DEVICES = 128


def table_rows(key, rise, level):
    first = jax.random.fold_in(key, 0)
    second = jax.random.fold_in(key, 1)
    third = jax.random.fold_in(key, 2)
    fifth = jax.random.fold_in(key, 4)
    total_rows = TAB_DEV * DEVICES
    place = jnp.arange(total_rows, dtype=jnp.float32)[:, None] / total_rows
    row_scale = level * jnp.exp(place * math.log(rise) + jax.random.uniform(first, (total_rows, 1), dtype=jnp.float32) * math.log(3.0))
    col_scale = jnp.exp(jax.random.uniform(second, (1, K), dtype=jnp.float32, minval=-1.15, maxval=1.15))
    owner_ids = jnp.arange(total_rows, dtype=jnp.int32) // TAB_DEV
    pairing = jax.random.permutation(fifth, K).astype(jnp.int32)
    heavy = pairing[owner_ids % K]
    boost = jnp.where(jnp.arange(K, dtype=jnp.int32)[None, :] == heavy[:, None], 8.0, 1.0).astype(jnp.float32)
    return (third, row_scale * col_scale * boost)


def draw_user_table(key, part):
    key = jax.random.fold_in(key, 11)
    third, scale = table_rows(key, 10.0, 0.0053)
    base = jax.random.normal(third, (TAB_DEV * DEVICES, K), dtype=jnp.float32)
    return (base * scale).astype(jnp.float32)


def draw_item_table(key, part):
    key = jax.random.fold_in(key, 12)
    third, scale = table_rows(key, 10.0, 0.0053)
    base = jax.random.normal(third, (TAB_DEV * DEVICES, K), dtype=jnp.float32)
    return (base * scale).astype(jnp.float32)


def place_ends(array, rng, least, top_value):
    extent = array.shape
    spot = [jax.random.randint(jax.random.fold_in(rng, axis), (), 0, extent[axis]) for axis in range(len(extent))]
    array = array.at[tuple(spot)].set(least)
    longest = extent.index(max(extent))
    spot[longest] = (spot[longest] + 1) % extent[longest]
    return array.at[tuple(spot)].set(top_value)


def block_levels(key, extent, shards, least, top_value):
    def one(dim, shards_of):
        steps = jax.random.uniform(jax.random.fold_in(jax.random.fold_in(key, 6), dim), (shards_of,), jnp.float32, least / len(shards), top_value / len(shards))
        return jnp.repeat(jnp.exp(steps), extent[dim] // shards_of).reshape((-1,) + (1,) * (len(extent) - dim - 1))

    loudness = one(*shards[0])
    for cut in shards[1:]:
        loudness = loudness * one(*cut)
    return loudness


def length_profile(number_of, total, most, slope):
    weights = [(1 << 20) // math.isqrt(grade ** slope) + 1 for grade in range(2, number_of + 1)]
    surplus, given = total - most - (number_of - 1), [1] * (number_of - 1)
    while surplus > 0:
        movable = [i for i in range(number_of - 1) if given[i] < most]
        pool, left = sum([weights[i] for i in movable]), surplus
        for i in movable:
            more = min(most - given[i], max(1, left * weights[i] // pool), surplus)
            given[i] = given[i] + more
            surplus = surplus - more
    return np.array([most] + given)


def uneven_parts(key, amount, total, limit, lean):
    if amount == 2:
        one = jax.random.randint(key, (), max(1, total - limit), min(limit, total - 1) + 1)
        return jnp.stack([one, total - one])
    lengths = jnp.asarray(length_profile(amount, total, limit, lean), jnp.int32)
    twos = (amount - 1) // 2
    giver, taker = lengths[1:1 + 2 * twos:2], lengths[2:2 + 2 * twos:2]
    slack = jnp.minimum(giver - 1, limit - taker)
    moved = jax.random.randint(jax.random.fold_in(key, 1), (twos,), 0, 1 << 20) % (slack + 1)
    lengths = lengths.at[1:1 + 2 * twos:2].set(giver - moved).at[2:2 + 2 * twos:2].set(taker + moved)
    return lengths[jax.random.permutation(jax.random.fold_in(key, 2), amount)]


def assign_block(stream_key, own, number, rows, count, top, most, skew):
    sequence = jax.random.permutation(stream_key, count)
    heavy_load, ordinary = shares(count, rows * top, most, skew, True), shares(count, rows * top, most, skew, False)
    places = jnp.arange(count)

    def named(lengths, offset_by):
        used = int((lengths > 0).sum())
        fixed = max(1, used // 4)
        shifted = fixed + (places - fixed + offset_by * (used - fixed)) % max(1, count - fixed)
        return jnp.zeros((count,), jnp.int32).at[sequence[jnp.where(places < fixed, places, shifted)]].set(jnp.asarray(lengths, jnp.int32))

    lengths = jnp.where(number % 4 == 0, named(heavy_load, number // 4), named(ordinary, number - number // 4 - 1))
    mixed = jax.random.permutation(jax.random.fold_in(own, 3), count)
    donor, receiver = mixed[0:count // 2 * 2:2], mixed[1:count // 2 * 2:2]
    margin = jnp.minimum(lengths[donor] - 1, most - lengths[receiver]) // 2
    margin = jnp.where((donor == sequence[0]) | (receiver == sequence[0]) | (lengths[receiver] == 0), 0, jnp.maximum(margin, 0))
    shifted = jax.random.randint(jax.random.fold_in(own, 4), (count // 2,), 0, 1 << 20) % (margin + 1)
    lengths = lengths.at[donor].add(-shifted).at[receiver].add(shifted)
    items = jnp.searchsorted(jnp.cumsum(lengths), jnp.arange(rows * top), side="right").astype(jnp.int32)
    listing = items.reshape(top, rows).T
    listing = listing[jax.random.permutation(jax.random.fold_in(own, 1), rows)]
    offset_by = jax.random.randint(jax.random.fold_in(own, 2), (rows, 1), 0, top)
    return jnp.take_along_axis(listing, (jnp.arange(top)[None, :] + offset_by) % top, axis=1)


def shares(number_of, total, reach, skew, full):
    weights = [(1 << 20) // math.isqrt(grade ** skew) + 1 for grade in range(1, number_of + 1)]
    largest = reach if full else min(reach, max(-(-total // number_of), total * weights[0] // sum(weights)))
    least = 1 if total - largest >= number_of - 1 else 0
    given, rest = [largest] + [least] * (number_of - 1), total - largest - least * (number_of - 1)
    while rest > 0:
        movable = [i for i in range(1, number_of) if given[i] < largest] or [i for i in range(1, number_of) if given[i] < reach]
        pool, left = sum([weights[i] for i in movable]), rest
        for i in movable:
            more = min(reach - given[i], max(1, left * weights[i] // pool), rest)
            given[i] = given[i] + more
            rest = rest - more
    return np.array(given)


def normal_values(key, dims, deviation, bound, cuts=(), kind=jnp.bfloat16):
    values = jax.random.normal(key, dims, jnp.float32) * deviation
    if len(cuts) > 0:
        values = block_levels(key, dims, cuts, -0.22, 0.18) * values
    return jnp.clip(values, min=-bound, max=bound).astype(kind)


def setup_inputs(seed: int = 0) -> dict:
    key_list = jax.random.split(jax.random.key(seed), 13)
    user_table = draw_user_table(jax.random.fold_in(key_list[12], 71), 0)
    item_table = draw_item_table(jax.random.fold_in(key_list[12], 71), 0)
    item_owner_keys = jax.random.split(jax.random.fold_in(key_list[2], 1), NNZ_ALL // NNZ_DEV)
    item_owner_turns = jax.random.permutation(jax.random.fold_in(key_list[2], 3), NNZ_ALL // NNZ_DEV)
    item_owner = jax.vmap(lambda own, number: assign_block(jax.random.fold_in(key_list[2], 2), own, number, NNZ_DEV, DEVICES, 1, CAP, 1))(item_owner_keys, item_owner_turns).reshape((NNZ_ALL, 1))
    item_row = place_ends(jax.random.randint(key_list[3], (NNZ_ALL,), 0, TAB_DEV), jax.random.fold_in(key_list[3], 1), 0, TAB_DEV - 1).astype(jnp.int32)
    user_confidence = jnp.clip(jnp.exp(math.log(8.0) - 2.7725887 * jax.random.uniform(key_list[4], (NNZ_ALL,), jnp.float32) ** block_levels(key_list[4], (NNZ_ALL,), ((0, 128),), -0.2, 0.2)), 0.5, 8.0)
    user_rating = normal_values(key_list[5], (NNZ_ALL,), 3.0, 12.0, ((0, 128),), jnp.float32)
    user_counts = jax.vmap(lambda own: uneven_parts(own, UB, LIVE, SEG_MAX, 2))(jax.random.split(key_list[6], BLOCKS_ALL)).reshape((BLOCKS_ALL, UB)).astype(jnp.int32)
    user_owner_keys = jax.random.split(jax.random.fold_in(key_list[7], 1), NNZ_ALL // NNZ_DEV)
    user_owner_turns = jax.random.permutation(jax.random.fold_in(key_list[7], 3), NNZ_ALL // NNZ_DEV)
    user_owner = jax.vmap(lambda own, number: assign_block(jax.random.fold_in(key_list[7], 2), own, number, NNZ_DEV, DEVICES, 1, CAP, 1))(user_owner_keys, user_owner_turns).reshape((NNZ_ALL, 1))
    user_row = place_ends(jax.random.randint(key_list[8], (NNZ_ALL,), 0, TAB_DEV), jax.random.fold_in(key_list[8], 1), 0, TAB_DEV - 1).astype(jnp.int32)
    item_confidence = jnp.clip(jnp.exp(math.log(8.0) - 2.7725887 * jax.random.uniform(key_list[9], (NNZ_ALL,), jnp.float32) ** block_levels(key_list[9], (NNZ_ALL,), ((0, 128),), -0.2, 0.2)), 0.5, 8.0)
    item_rating = normal_values(key_list[10], (NNZ_ALL,), 3.0, 12.0, ((0, 128),), jnp.float32)
    item_counts = jax.vmap(lambda own: uneven_parts(own, UB, LIVE, SEG_MAX, 2))(jax.random.split(key_list[11], BLOCKS_ALL)).reshape((BLOCKS_ALL, UB)).astype(jnp.int32)
    return dict(user_table=user_table, item_table=item_table, item_owner=item_owner, item_row=item_row, user_confidence=user_confidence, user_rating=user_rating, user_counts=user_counts, user_owner=user_owner, user_row=user_row, item_confidence=item_confidence, item_rating=item_rating, item_counts=item_counts)


ridge_weight = 1.0
global_weight = 256.0
guard_eps = 1e-6


def apply_system(system, vector):
    return jnp.einsum('bkl,bl->bk', system, vector, precision=lax.Precision.HIGHEST)


def conjugate(system, right_side, warm_start):
    iterate = warm_start
    resid = right_side - apply_system(system, iterate)
    direction = resid
    norm_now = jnp.sum(resid * resid, -1, keepdims=True)
    for iteration in range(ITERS):
        images = apply_system(system, direction)
        step_size = norm_now / (jnp.sum(direction * images, -1, keepdims=True) + guard_eps)
        iterate = iterate + step_size * direction
        resid = resid - step_size * images
        norm_next = jnp.sum(resid * resid, -1, keepdims=True)
        direction = resid + (norm_next / (norm_now + guard_eps)) * direction
        norm_now = norm_next
    return iterate


def solve_blocks(fetched, confidence, rating, counts, warm_start, global_gram, gram_scale):
    block_count, block_rows, width = fetched.shape
    seg_ends = jnp.cumsum(counts.astype(jnp.int32), -1, dtype=jnp.int32).astype(jnp.int32)
    begins = (seg_ends - counts.astype(jnp.int32)).astype(jnp.int32)
    position = jnp.arange(block_rows, dtype=jnp.int32)
    inside = (position[None, None, :] >= begins[..., None]) & (position[None, None, :] < seg_ends[..., None])
    weights = jnp.where(inside, confidence[:, None, :], jnp.zeros((), confidence.dtype))
    fetched_wide = fetched.astype(jnp.float32)
    weighted = (weights[..., None] * fetched_wide[:, None]).astype(jnp.bfloat16)
    local_gram = jnp.einsum('bsjk,bjl->bskl', weighted.astype(jnp.float32), fetched_wide, precision=lax.Precision.HIGHEST)
    right_side = jnp.einsum('bsj,bjk->bsk', weights * rating[:, None, :], fetched_wide, precision=lax.Precision.HIGHEST)
    system = ridge_weight * jnp.eye(width, dtype=jnp.float32) + gram_scale * global_gram + local_gram
    solved = conjugate(system.reshape(-1, width, width), right_side.reshape(-1, width), warm_start.reshape(-1, width))
    return solved.reshape(block_count, -1, width)


def half_step(own_table, source, owner, rows_local, confidence, rating, counts):
    devices = N_GX * N_GY
    global_gram = jnp.dot(source.T, source, precision=lax.Precision.HIGHEST, preferred_element_type=jnp.float32)
    gram_scale = global_weight / (TAB_DEV * devices)
    source_narrow = source.astype(jnp.bfloat16)
    global_ids = (owner[:, 0].astype(jnp.int32) * TAB_DEV + rows_local.astype(jnp.int32)).astype(jnp.int32)
    fetched = source_narrow[global_ids].reshape(devices, BLOCKS, BLOCK_ROWS, K)
    conf_all = confidence.reshape(devices, BLOCKS, BLOCK_ROWS)
    rating_all = rating.reshape(devices, BLOCKS, BLOCK_ROWS)
    counts_all = counts.reshape(devices, BLOCKS, UB)
    tables = own_table.reshape(devices, TAB_DEV, K)
    starts = tables[:, :BATCH_DEV].reshape(devices, BLOCKS, UB, K)

    def one_device(inputs):
        return solve_blocks(inputs[0], inputs[1], inputs[2], inputs[3], inputs[4], global_gram, gram_scale)

    renewed = lax.map(one_device, (fetched, conf_all, rating_all, counts_all, starts))
    updated = jnp.concatenate([renewed.reshape(devices, BATCH_DEV, K).astype(own_table.dtype), tables[:, BATCH_DEV:]], 1)
    return updated.reshape(-1, K)


def reference(user_table, item_table, item_owner, item_row, user_confidence, user_rating, user_counts, user_owner, user_row, item_confidence, item_rating, item_counts):
    new_users = half_step(user_table, item_table, item_owner, item_row, user_confidence, user_rating, user_counts)
    new_items = half_step(item_table, new_users, user_owner, user_row, item_confidence, item_rating, item_counts)
    return (new_users, new_items)
```

```python
import functools

import jax
import jax.numpy as jnp
from jax import lax
from jax.experimental import pallas as pl
from jax.experimental.pallas import tpu as pltpu
from jax.sharding import PartitionSpec as P

ITERS = 8
AXES = ("gx", "gy")
LIVE = 112
PAD = 64
CAP = 60
LANES = 128

ridge_weight = 1.0
global_weight = 256.0
guard_eps = 1e-06


def bucket_kernel(chunks, owner_ref, row_ref, request_ref, slot_ref):
    sub = lax.broadcasted_iota(jnp.int32, (LANES, LANES), 0)
    lane = lax.broadcasted_iota(jnp.int32, (LANES, LANES), 1)
    below = jnp.where(sub < lane, 1.0, 0.0)
    prefix = jnp.concatenate([below, jnp.ones_like(below)], 1).astype(jnp.bfloat16)
    place = sub % PAD
    first_half = sub < PAD
    group = 8
    halves = []
    for half in range(2):

        def step(g, state):
            carry, wanted = state
            start = pl.multiple_of(half * chunks + g * group, group)
            owners = owner_ref[pl.ds(start, group), :]
            rows = row_ref[pl.ds(start, group), :]
            live = lax.broadcasted_iota(jnp.int32, owners.shape, 1) < LIVE
            masked = jnp.where(live, owners, -1)
            high = (rows // PAD).astype(jnp.float32)
            low = (rows % PAD).astype(jnp.float32)
            if half == 1:
                high, low = low, high
            hot = []
            counted = []
            for c in range(group):
                hit = sub == masked[c : c + 1, :]
                hot.append(jnp.where(hit, 1.0, 0.0))
                counted.append(
                    jnp.dot(hot[c].astype(jnp.bfloat16), prefix, preferred_element_type=jnp.float32)
                )
            ranks = []
            for c in range(group):
                before = counted[c][:, :LANES] + carry
                ranks.append(jnp.sum(before * hot[c], 0, keepdims=True).astype(jnp.int32))
                carry = carry + counted[c][:, LANES:]
            for c in range(group):
                value = jnp.where(first_half, high[c : c + 1, :], low[c : c + 1, :])
                put = jnp.where(place == ranks[c], value, 0.0).astype(jnp.bfloat16)
                wanted = wanted + lax.dot_general(
                    hot[c].astype(jnp.bfloat16),
                    put,
                    (((1,), (1,)), ((), ())),
                    preferred_element_type=jnp.float32,
                )
            slot_ref[pl.ds(start, group), :] = owners * PAD + jnp.concatenate(ranks, 0)
            return carry, wanted

        zero = jnp.zeros((LANES, LANES), jnp.float32)
        _, wanted = lax.fori_loop(0, chunks // group, step, (zero, zero))
        halves.append(wanted * PAD + pltpu.roll(wanted, PAD, 1))
    request_ref[...] = jnp.where(lane < PAD, halves[0], halves[1])


def bucket(owner, rows):
    chunks = owner.shape[0] // 2
    return pl.pallas_call(
        functools.partial(bucket_kernel, chunks),
        out_shape=(
            jax.ShapeDtypeStruct((LANES, LANES), jnp.float32),
            jax.ShapeDtypeStruct(owner.shape, jnp.int32),
        ),
        compiler_params=pltpu.CompilerParams(vmem_limit_bytes=32 << 20),
        name="bucket",
    )(owner, rows)


def gather_kernel(half, per_step, request_ref, table_ref, extra_ref, out_ref, wide):
    base = pl.program_id(0) * per_step

    def one(s, state):
        buffer = wide.at[s % 2]
        for i in range(CAP):
            index = request_ref[base + s, half * PAD + i]
            buffer[pl.ds(i, 1), :] = table_ref[pl.ds(index, 1), :]
        buffer[CAP:, :] = extra_ref[s]
        out_ref[s] = buffer[...].astype(jnp.bfloat16)
        return state

    lax.fori_loop(0, per_step, one, 0)


def gather(half, requests, table, extra):
    devices = requests.shape[0]
    steps = 8
    per_step = devices // steps
    return pl.pallas_call(
        functools.partial(gather_kernel, half, per_step),
        grid=(steps,),
        in_specs=[
            pl.BlockSpec(memory_space=pltpu.SMEM),
            pl.BlockSpec(table.shape, lambda i: (0, 0)),
            pl.BlockSpec((per_step,) + extra.shape[1:], lambda i: (i, 0, 0)),
        ],
        out_specs=pl.BlockSpec((per_step, PAD, LANES), lambda i: (i, 0, 0)),
        out_shape=jax.ShapeDtypeStruct((devices, PAD, LANES), jnp.bfloat16),
        scratch_shapes=[pltpu.VMEM((2, PAD, LANES), jnp.float32)],
        compiler_params=pltpu.CompilerParams(vmem_limit_bytes=32 << 20),
        name="gather_rows",
    )(requests, table, extra)


def solve_kernel(
    blocks,
    gram_scale,
    slot_ref,
    count_ref,
    reply_ref,
    conf_ref,
    rating_ref,
    warm_ref,
    gram_ref,
    out_ref,
    wide,
    weight_wide,
    rows,
    turned,
    weighted,
    inside,
    x_ref,
    r_ref,
    p_ref,
    g_ref,
):
    sub = lax.broadcasted_iota(jnp.int32, (8, LANES), 0)
    lane = lax.broadcasted_iota(jnp.int32, (8, LANES), 1)
    top = sub < 4

    def fold(value):
        return value + pltpu.roll(value, 4, 0)

    def split(value):
        head = value.astype(jnp.bfloat16).astype(jnp.float32)
        return jnp.where(top, head, value - head).astype(jnp.bfloat16)

    def widen(i, state):
        start = pl.multiple_of(i * 512, 512)
        wide[pl.ds(start, 512), :] = reply_ref[pl.ds(start, 512), :].astype(jnp.float32)
        return state

    lax.fori_loop(0, reply_ref.shape[0] // 512, widen, 0)
    conf_turned = jnp.concatenate(
        [conf_ref[...], jnp.zeros((LANES - blocks, LANES), jnp.float32)], 0
    ).T
    for b in range(blocks):
        weight_wide[b] = jnp.broadcast_to(conf_turned[:, b : b + 1], (LANES, LANES))
    rows[...] = jnp.zeros_like(rows)

    def build(b, state):
        buffer = rows.at[b % 2]
        for t in range(LIVE):
            buffer[pl.ds(t, 1), :] = wide[pl.ds(slot_ref[b, t], 1), :]
        fetched = buffer[...]
        turned[b] = fetched.T.astype(jnp.bfloat16)
        weighted[b] = (weight_wide[b] * fetched).astype(jnp.bfloat16)
        end0 = count_ref[b, 0]
        end1 = end0 + count_ref[b, 1]
        end2 = end1 + count_ref[b, 2]
        end3 = end2 + count_ref[b, 3]
        which = sub % 4
        begin = jnp.where(which == 0, 0, jnp.where(which == 1, end0, jnp.where(which == 2, end1, end2)))
        end = jnp.where(which == 0, end0, jnp.where(which == 1, end1, jnp.where(which == 2, end2, end3)))
        mask = jnp.where((lane >= begin) & (lane < end), 1.0, 0.0)
        inside[b] = mask
        target = conf_ref[pl.ds(b, 1), :] * rating_ref[pl.ds(b, 1), :] * mask
        right = jnp.dot(
            split(target), fetched.astype(jnp.bfloat16), preferred_element_type=jnp.float32
        )
        r_ref[b] = fold(right)
        start = warm_ref[b]
        x_ref[b] = start
        p_ref[b] = start
        return state

    lax.fori_loop(0, blocks, build, 0)

    gram = gram_ref[...] * gram_scale
    gram_head = gram.astype(jnp.bfloat16)
    gram_tail = (gram - gram_head.astype(jnp.float32)).astype(jnp.bfloat16)
    gram_both = jnp.concatenate([gram_head, gram_tail], 1)
    group = 16

    def apply_system(g):
        ids = [g * group + c for c in range(group)]
        dirs = [p_ref[b] for b in ids]
        cut = [split(d) for d in dirs]
        shared = jnp.dot(jnp.concatenate(cut, 0), gram_both, preferred_element_type=jnp.float32)
        along = [
            fold(jnp.dot(cut[c], turned[ids[c]], preferred_element_type=jnp.float32))
            for c in range(group)
        ]
        back = [
            jnp.dot(
                split(along[c] * inside[ids[c]]),
                weighted[ids[c]],
                preferred_element_type=jnp.float32,
            )
            for c in range(group)
        ]
        images = []
        for c in range(group):
            part = shared[8 * c : 8 * c + 8]
            images.append(
                fold(back[c] + part[:, :LANES] + part[:, LANES:]) + ridge_weight * dirs[c]
            )
        return ids, dirs, images

    for g in range(blocks // group):
        ids, dirs, images = apply_system(g)
        for c in range(group):
            resid = r_ref[ids[c]] - images[c]
            r_ref[ids[c]] = resid
            p_ref[ids[c]] = resid
            g_ref[ids[c]] = jnp.broadcast_to(
                jnp.sum(resid * resid, -1, keepdims=True), (8, LANES)
            )

    def iterate(i, state):
        for g in range(blocks // group):
            ids, dirs, images = apply_system(g)
            for c in range(group):
                b = ids[c]
                norm_now = g_ref[b]
                step_size = norm_now / (
                    jnp.sum(dirs[c] * images[c], -1, keepdims=True) + guard_eps
                )
                x_ref[b] = x_ref[b] + step_size * dirs[c]
                resid = r_ref[b] - step_size * images[c]
                r_ref[b] = resid
                norm_next = jnp.sum(resid * resid, -1, keepdims=True)
                p_ref[b] = resid + norm_next / (norm_now + guard_eps) * dirs[c]
                g_ref[b] = jnp.broadcast_to(norm_next, (8, LANES))
        return state

    lax.fori_loop(0, ITERS, iterate, 0)
    out_ref[...] = x_ref[...]


def solve(slots, counts, replies, confidence, rating, warm_start, gram, gram_scale):
    blocks = counts.shape[0]
    doubled = jnp.concatenate([warm_start.reshape(blocks, 4, LANES)] * 2, 1)
    vmem = pl.BlockSpec(memory_space=pltpu.VMEM)
    smem = pl.BlockSpec(memory_space=pltpu.SMEM)
    state = pltpu.VMEM((blocks, 8, LANES), jnp.float32)
    solved = pl.pallas_call(
        functools.partial(solve_kernel, blocks, gram_scale),
        in_specs=[smem, smem, vmem, vmem, vmem, vmem, vmem],
        out_specs=vmem,
        out_shape=jax.ShapeDtypeStruct((blocks, 8, LANES), jnp.float32),
        scratch_shapes=[
            pltpu.VMEM(replies.shape, jnp.float32),
            pltpu.VMEM((blocks, LANES, LANES), jnp.float32),
            pltpu.VMEM((2, LANES, LANES), jnp.float32),
            pltpu.VMEM((blocks, LANES, LANES), jnp.bfloat16),
            pltpu.VMEM((blocks, LANES, LANES), jnp.bfloat16),
            state,
            state,
            state,
            state,
            state,
        ],
        compiler_params=pltpu.CompilerParams(vmem_limit_bytes=48 << 20),
        name="solve_rows",
    )(slots, counts, replies, confidence, rating, doubled, gram)
    return solved[:, :4].reshape(blocks * 4, LANES)


def exchange(values):
    return lax.all_to_all(values, AXES, split_axis=0, concat_axis=0, tiled=True)


def local_gram(table):
    return jnp.dot(
        table.T, table, precision=lax.Precision.HIGH, preferred_element_type=jnp.float32
    )


def three_parts(values):
    head = values.astype(jnp.bfloat16).astype(jnp.float32)
    rest = values - head
    middle = rest.astype(jnp.bfloat16).astype(jnp.float32)
    return head, middle, rest - middle


def shards(
    user_table,
    item_table,
    item_owner,
    item_row,
    user_confidence,
    user_rating,
    user_counts,
    user_owner,
    user_row,
    item_confidence,
    item_rating,
    item_counts,
):
    devices = lax.axis_size(AXES)
    tab_rows, width = user_table.shape
    blocks = user_counts.shape[0]
    batch = blocks * user_counts.shape[1]
    gram_scale = global_weight / (tab_rows * devices)

    def by_block(values):
        return values.reshape(blocks, -1)

    requests, slots = bucket(
        jnp.concatenate([by_block(item_owner), by_block(user_owner)], 0),
        jnp.concatenate([by_block(item_row), by_block(user_row)], 0),
    )
    item_gram = local_gram(item_table)
    came = exchange(jnp.concatenate([requests, item_gram], 1)[:, None, :])[:, 0]
    wanted = came[:, :width].astype(jnp.int32)
    gram_row = jnp.sum(came[:, width:], 0)
    extra = jnp.stack(three_parts(gram_row) + (jnp.zeros_like(gram_row),), 0)
    replies = exchange(
        gather(0, wanted, item_table, jnp.broadcast_to(extra[None], (devices, 4, width)))
    )
    item_gram = jnp.sum(replies[:, CAP:].astype(jnp.float32), 1)
    renewed = solve(
        slots[:blocks],
        user_counts,
        replies.reshape(-1, width),
        by_block(user_confidence),
        by_block(user_rating),
        user_table[:batch],
        item_gram,
        gram_scale,
    )
    new_users = jnp.concatenate([renewed, user_table[batch:]], 0)

    user_gram = local_gram(new_users)
    extra = jnp.stack(three_parts(user_gram) + (jnp.zeros_like(user_gram),), 1)
    replies = exchange(gather(1, wanted, new_users, extra))
    gram_row = jnp.sum(replies[:, CAP:].astype(jnp.float32), (0, 1))
    user_gram = exchange(jnp.broadcast_to(gram_row[None, None], (devices, 1, width)))[:, 0]
    renewed = solve(
        slots[blocks:],
        item_counts,
        replies.reshape(-1, width),
        by_block(item_confidence),
        by_block(item_rating),
        item_table[:batch],
        user_gram,
        gram_scale,
    )
    new_items = jnp.concatenate([renewed, item_table[batch:]], 0)
    return (new_users, new_items)


def solution(mesh):
    spec = P(AXES, None)
    flat = P(AXES)
    in_specs = (spec, spec, spec, flat, flat, flat, spec, spec, flat, flat, flat, spec)
    return jax.shard_map(
        shards, mesh=mesh, in_specs=in_specs, out_specs=(spec, spec), check_vma=False
    )
```

```python
import functools

import jax
import jax.numpy as jnp
from jax import lax
from jax.experimental import pallas as pl
from jax.experimental.pallas import tpu as pltpu
from jax.sharding import PartitionSpec as P

ITERS = 8
AXES = ("gx", "gy")
LIVE = 112
PAD = 64
CAP = 60
PATCH = 14
SLOT = 16
EARLY = 48
EAGER = 6
TOGETHER = 4
LANES = 128

ridge_weight = 1.0
global_weight = 256.0
guard_eps = 1e-06


def bucket_kernel(batch, owner0, row0, owner1, row1, gram_ref, request_ref, slot0, slot1, place_ref):
    chunks = owner0.shape[0]
    sub = lax.broadcasted_iota(jnp.int32, (LANES, LANES), 0)
    lane = lax.broadcasted_iota(jnp.int32, (LANES, LANES), 1)
    below = jnp.where(sub < lane, 1.0, 0.0)
    prefix = jnp.concatenate([below, jnp.ones_like(below)], 1).astype(jnp.bfloat16)
    place = sub % PAD
    first_half = sub < PAD
    group = 8
    zero = jnp.zeros((LANES, LANES), jnp.float32)

    def step(half, g, state):
        carry, wanted = state
        start = pl.multiple_of(g * group, group)
        owners = (owner0, owner1)[half][pl.ds(start, group), :]
        rows = (row0, row1)[half][pl.ds(start, group), :]
        position = lax.broadcasted_iota(jnp.int32, owners.shape, 1)
        masked = jnp.where(position < LIVE, owners, -1)
        unit = jnp.where(rows < batch, 1.0, float(PAD)) if half == 1 else None
        hot = []
        counted = []
        for c in range(group):
            hit = sub == masked[c : c + 1, :]
            hot.append(jnp.where(hit, 1.0, 0.0))
            tally = hot[c] if half == 0 else jnp.where(hit, unit[c : c + 1, :], 0.0)
            counted.append(
                jnp.dot(tally.astype(jnp.bfloat16), prefix, preferred_element_type=jnp.float32)
            )
        ranks = []
        for c in range(group):
            before = counted[c][:, :LANES] + carry
            ranks.append(jnp.sum(before * hot[c], 0, keepdims=True).astype(jnp.int32))
            carry = carry + counted[c][:, LANES:]
        ranks = jnp.concatenate(ranks, 0)
        if half == 1:
            ranks = jnp.where(rows < batch, ranks % PAD, CAP - 1 - ranks // PAD)
        high = (rows // PAD).astype(jnp.float32)
        low = (rows % PAD).astype(jnp.float32)
        if half == 1:
            high, low = low, high
        lane_row = position.astype(jnp.float32)
        for c in range(group):
            chosen = place == ranks[c : c + 1, :]
            value = jnp.where(first_half, high[c : c + 1, :], low[c : c + 1, :])
            put = jnp.where(chosen, value, 0.0).astype(jnp.bfloat16)
            if half == 1:
                spot = jnp.where(
                    first_half, lane_row[c : c + 1, :], (g * group + c).astype(jnp.float32)
                )
                put = jnp.concatenate(
                    [put, jnp.where(chosen, spot, 0.0).astype(jnp.bfloat16)], 0
                )
            wanted = wanted + lax.dot_general(
                hot[c].astype(jnp.bfloat16),
                put,
                (((1,), (1,)), ((), ())),
                preferred_element_type=jnp.float32,
            )
        if half == 0:
            slot0[pl.ds(start, group), :] = owners * PAD + ranks
        else:
            slot1[pl.ds(start, group), :] = owners * EARLY + jnp.where(
                ranks < PATCH, EARLY - 1, ranks - PATCH
            )
        return carry, wanted

    steps = chunks // group
    _, first = lax.fori_loop(0, steps, functools.partial(step, 0), (zero, zero))
    wide = jnp.concatenate([zero, zero], 1)
    tally, second = lax.fori_loop(0, steps, functools.partial(step, 1), (zero, wide))
    spots = second[:, LANES:]
    second = second[:, :LANES]
    first = first * PAD + pltpu.roll(first, PAD, 1)
    second = second * PAD + pltpu.roll(second, PAD, 1)
    spots = spots + pltpu.roll(spots, PAD, 1) * LANES
    renewed = tally.astype(jnp.int32) % PAD
    most = jnp.max(renewed).astype(jnp.float32)
    request = jnp.where(lane < PAD, first, second)
    request_ref[:, :LANES] = jnp.where(lane == LANES - 1, most, request)
    request_ref[:, LANES:] = gram_ref[...]
    others = tally.astype(jnp.int32) // PAD
    used = (lane < renewed) | (lane >= CAP - others)
    places = jnp.where(used, spots.astype(jnp.int32), chunks * LANES)
    looked = jnp.where(others > CAP - PATCH, PATCH, jnp.minimum(renewed, PATCH))
    places = jnp.where(lane == PAD - 2, looked, places)
    place_ref[...] = jnp.where(lane == PAD - 1, renewed, places)


def bucket(owner0, row0, owner1, row1, gram, batch):
    slots = jax.ShapeDtypeStruct(owner0.shape, jnp.int32)
    return pl.pallas_call(
        functools.partial(bucket_kernel, batch),
        out_shape=(
            jax.ShapeDtypeStruct((LANES, 2 * LANES), jnp.float32),
            slots,
            slots,
            jax.ShapeDtypeStruct((LANES, LANES), jnp.int32),
        ),
        compiler_params=pltpu.CompilerParams(vmem_limit_bytes=32 << 20),
        name="bucket",
    )(owner0, row0, owner1, row1, gram)


def gather_kernel(first, count, per_step, request_ref, table_ref, *refs):
    out_ref, wide = refs[-2:]
    base = pl.program_id(0) * per_step
    depth = wide.shape[1]
    last = jnp.zeros((depth - count, LANES), jnp.float32)
    if len(refs) == 3:
        row = refs[0][...]
        head = row.astype(jnp.bfloat16).astype(jnp.float32)
        last = jnp.concatenate([head, row - head, last[2:]], 0)
    for k in range(2):
        wide[k, count:, :] = last

    def one(s, state):
        buffer = wide.at[s % 2]
        for i in range(count):
            index = request_ref[base + s, first + i]
            buffer[pl.ds(i, 1), :] = table_ref[pl.ds(index, 1), :]
        out_ref[s] = buffer[...].astype(jnp.bfloat16)
        return state

    lax.fori_loop(0, per_step, one, 0)


def gather(first, count, depth, requests, table, extra=None):
    devices = requests.shape[0]
    steps = 8
    per_step = devices // steps
    more = () if extra is None else (extra,)
    return pl.pallas_call(
        functools.partial(gather_kernel, first, count, per_step),
        grid=(steps,),
        in_specs=[
            pl.BlockSpec(memory_space=pltpu.SMEM),
            pl.BlockSpec(table.shape, lambda i: (0, 0)),
        ]
        + [pl.BlockSpec(extra.shape, lambda i: (0, 0)) for extra in more],
        out_specs=pl.BlockSpec((per_step, depth, LANES), lambda i: (i, 0, 0)),
        out_shape=pltpu.HBM((devices, depth, LANES), jnp.bfloat16),
        scratch_shapes=[pltpu.VMEM((2, depth, LANES), jnp.float32)],
        compiler_params=pltpu.CompilerParams(vmem_limit_bytes=32 << 20),
        name="gather_rows",
    )(requests, table, *more)


def unsort_kernel(slot_ref, reply_ref, out_ref, wide):
    widen(reply_ref, wide)

    def one(b, state):
        for t in range(LIVE):
            out_ref[b, pl.ds(t, 1), :] = wide[pl.ds(slot_ref[b, t], 1), :]
        out_ref[b, LIVE:, :] = jnp.zeros((LANES - LIVE, LANES), jnp.float32)
        return state

    lax.fori_loop(0, out_ref.shape[0], one, 0)


def unsort(slots, replies):
    blocks = slots.shape[0]
    return pl.pallas_call(
        unsort_kernel,
        in_specs=[pl.BlockSpec(memory_space=pltpu.SMEM), pl.BlockSpec(memory_space=pltpu.VMEM)],
        out_specs=pl.BlockSpec(memory_space=pltpu.VMEM),
        out_shape=pltpu.VMEM((blocks, LANES, LANES), jnp.float32),
        scratch_shapes=[pltpu.VMEM(replies.shape, jnp.float32)],
        compiler_params=pltpu.CompilerParams(vmem_limit_bytes=32 << 20),
        name="unsort_rows",
    )(slots, replies)


def fold(value):
    return value + pltpu.roll(value, 4, 0)


def split(value):
    top = lax.broadcasted_iota(jnp.int32, value.shape, 0) < 4
    head = value.astype(jnp.bfloat16).astype(jnp.float32)
    return jnp.where(top, head, value - head).astype(jnp.bfloat16)


def widen(source, target):
    step = 512

    def one(i, state):
        start = pl.multiple_of(i * step, step)
        target[pl.ds(start, step), :] = source[pl.ds(start, step), :].astype(jnp.float32)
        return state

    lax.fori_loop(0, source.shape[0] // step, one, 0)


def spread_weights(conf_ref, weight_wide):
    blocks = conf_ref.shape[0]
    conf_turned = jnp.concatenate(
        [conf_ref[...], jnp.zeros((LANES - blocks, LANES), jnp.float32)], 0
    ).T
    for b in range(blocks):
        weight_wide[b] = jnp.broadcast_to(conf_turned[:, b : b + 1], (LANES, LANES))


def build_blocks(
    first, rows, count_ref, conf_ref, rating_ref, weight_wide, turned, weighted, inside, right
):
    sub = lax.broadcasted_iota(jnp.int32, (8, LANES), 0)
    lane = lax.broadcasted_iota(jnp.int32, (8, LANES), 1)
    which = sub % 4
    sums = []
    for c, fetched in enumerate(rows):
        b = first + c
        turned[b] = fetched.T.astype(jnp.bfloat16)
        weighted[b] = (weight_wide[b] * fetched).astype(jnp.bfloat16)
        end0 = count_ref[b, 0]
        end1 = end0 + count_ref[b, 1]
        end2 = end1 + count_ref[b, 2]
        end3 = end2 + count_ref[b, 3]
        begin = jnp.where(which < 2, jnp.where(which == 0, 0, end0), jnp.where(which == 2, end1, end2))
        end = jnp.where(which < 2, jnp.where(which == 0, end0, end1), jnp.where(which == 2, end2, end3))
        mask = jnp.where((lane >= begin) & (lane < end), 1.0, 0.0)
        inside[b] = mask
        target = conf_ref[pl.ds(b, 1), :] * rating_ref[pl.ds(b, 1), :] * mask
        sums.append(
            jnp.dot(split(target), fetched.astype(jnp.bfloat16), preferred_element_type=jnp.float32)
        )
    for c, part in enumerate(sums):
        right[first + c] = fold(part)


def start_from(warm_ref, x_ref, p_ref):
    for b in range(x_ref.shape[0]):
        warm = warm_ref[pl.ds(4 * b, 4), :]
        both = jnp.concatenate([warm, warm], 0)
        x_ref[b] = both
        p_ref[b] = both


def give(x_ref, out_ref):
    for b in range(x_ref.shape[0]):
        out_ref[pl.ds(4 * b, 4), :] = x_ref[b, :4, :]


def conjugate(gram, turned, weighted, inside, x_ref, r_ref, p_ref, g_ref):
    blocks = x_ref.shape[0]
    gram_head = gram.astype(jnp.bfloat16)
    gram_tail = (gram - gram_head.astype(jnp.float32)).astype(jnp.bfloat16)
    gram_both = jnp.concatenate([gram_head, gram_tail], 1)
    group = 16

    def apply_system(g):
        ids = [g * group + c for c in range(group)]
        dirs = [p_ref[b] for b in ids]
        cut = [split(d) for d in dirs]
        shared = jnp.dot(jnp.concatenate(cut, 0), gram_both, preferred_element_type=jnp.float32)
        along = [
            fold(jnp.dot(cut[c], turned[ids[c]], preferred_element_type=jnp.float32))
            for c in range(group)
        ]
        back = [
            jnp.dot(
                split(along[c] * inside[ids[c]]),
                weighted[ids[c]],
                preferred_element_type=jnp.float32,
            )
            for c in range(group)
        ]
        images = []
        for c in range(group):
            part = shared[8 * c : 8 * c + 8]
            images.append(
                fold(back[c] + part[:, :LANES] + part[:, LANES:]) + ridge_weight * dirs[c]
            )
        return ids, dirs, images

    for g in range(blocks // group):
        ids, dirs, images = apply_system(g)
        for c in range(group):
            resid = r_ref[ids[c]] - images[c]
            r_ref[ids[c]] = resid
            p_ref[ids[c]] = resid
            g_ref[ids[c]] = jnp.broadcast_to(
                jnp.sum(resid * resid, -1, keepdims=True), (8, LANES)
            )

    def iterate(i, state):
        for g in range(blocks // group):
            ids, dirs, images = apply_system(g)
            for c in range(group):
                b = ids[c]
                norm_now = g_ref[b]
                step_size = norm_now / (
                    jnp.sum(dirs[c] * images[c], -1, keepdims=True) + guard_eps
                )
                x_ref[b] = x_ref[b] + step_size * dirs[c]
                resid = r_ref[b] - step_size * images[c]
                r_ref[b] = resid
                norm_next = jnp.sum(resid * resid, -1, keepdims=True)
                p_ref[b] = resid + norm_next / (norm_now + guard_eps) * dirs[c]
                g_ref[b] = jnp.broadcast_to(norm_next, (8, LANES))
        return state

    lax.fori_loop(0, ITERS, iterate, 0)


def solve_users_kernel(
    gram_scale,
    slot_ref,
    wanted_ref,
    count_ref,
    reply_ref,
    conf_ref,
    rating_ref,
    table_ref,
    still_ref,
    out_ref,
    patch_ref,
    wide,
    weight_wide,
    rows,
    turned,
    weighted,
    inside,
    x_ref,
    r_ref,
    p_ref,
    g_ref,
):
    blocks = conf_ref.shape[0]
    batch = 4 * blocks
    widen(reply_ref, wide)
    spread_weights(conf_ref, weight_wide)
    rows[...] = jnp.zeros_like(rows)

    def build(g, state):
        first = g * TOGETHER
        for c in range(TOGETHER):
            for t in range(LIVE):
                rows[c, pl.ds(t, 1), :] = wide[pl.ds(slot_ref[first + c, t], 1), :]
        build_blocks(
            first,
            [rows[c] for c in range(TOGETHER)],
            count_ref,
            conf_ref,
            rating_ref,
            weight_wide,
            turned,
            weighted,
            inside,
            r_ref,
        )
        return state

    lax.fori_loop(0, blocks // TOGETHER, build, 0)
    start_from(table_ref, x_ref, p_ref)
    gram = wide[pl.ds(CAP, LANES, stride=PAD), :] + wide[pl.ds(CAP + 1, LANES, stride=PAD), :]
    conjugate(gram * gram_scale, turned, weighted, inside, x_ref, r_ref, p_ref, g_ref)
    give(x_ref, out_ref)

    table = wide.at[pl.ds(0, table_ref.shape[0])]
    solved = out_ref[...]
    table[pl.ds(0, batch), :] = solved
    step = 64

    def copy(i, state):
        start = pl.multiple_of(batch + i * step, step)
        table[pl.ds(start, step), :] = table_ref[pl.ds(start, step), :]
        return state

    lax.fori_loop(0, (table_ref.shape[0] - batch) // step, copy, 0)
    head = solved.astype(jnp.bfloat16)
    rest = (solved - head.astype(jnp.float32)).astype(jnp.bfloat16)
    head_turned = head.astype(jnp.float32).T.astype(jnp.bfloat16)
    cross = jnp.dot(head_turned, rest, preferred_element_type=jnp.float32)
    gram = jnp.dot(head_turned, head, preferred_element_type=jnp.float32) + cross + cross.T
    rows[0] = still_ref[...] + gram

    def one(o, state):
        buffer = rows.at[1, pl.ds(pl.multiple_of(o % 2 * SLOT, SLOT), SLOT)]
        for i in range(PATCH):
            buffer[pl.ds(i, 1), :] = table[pl.ds(wanted_ref[o, PAD + i], 1), :]
        share = rows[0, pl.ds(o, 1), :]
        top = share.astype(jnp.bfloat16).astype(jnp.float32)
        buffer[pl.ds(PATCH, 1), :] = top
        buffer[pl.ds(PATCH + 1, 1), :] = share - top
        patch_ref[o] = buffer[...].astype(jnp.bfloat16)
        return state

    lax.fori_loop(0, wanted_ref.shape[0], one, 0)


def solve_users(slots, wanted, counts, replies, confidence, rating, table, still, gram_scale):
    blocks = confidence.shape[0]
    vmem = pl.BlockSpec(memory_space=pltpu.VMEM)
    smem = pl.BlockSpec(memory_space=pltpu.SMEM)
    state = pltpu.VMEM((blocks, 8, LANES), jnp.float32)
    matrices = pltpu.VMEM((blocks, LANES, LANES), jnp.bfloat16)
    return pl.pallas_call(
        functools.partial(solve_users_kernel, gram_scale),
        in_specs=[smem] * 3 + [vmem] * 5,
        out_specs=[vmem, vmem],
        out_shape=[
            jax.ShapeDtypeStruct((4 * blocks, LANES), jnp.float32),
            pltpu.HBM((wanted.shape[0], SLOT, LANES), jnp.bfloat16),
        ],
        scratch_shapes=[
            pltpu.VMEM(replies.shape, jnp.float32),
            pltpu.VMEM((blocks, LANES, LANES), jnp.float32),
            pltpu.VMEM((TOGETHER, LANES, LANES), jnp.float32),
            matrices,
            matrices,
        ]
        + [state] * 5,
        compiler_params=pltpu.CompilerParams(vmem_limit_bytes=48 << 20),
        name="solve_users",
    )(slots, wanted, counts, replies, confidence, rating, table, still)


def build_items_kernel(
    place_ref,
    count_ref,
    rows_ref,
    patch_ref,
    more_ref,
    conf_ref,
    rating_ref,
    turned,
    weighted,
    inside,
    right,
    wide,
    more_narrow,
    more_wide,
    weight_wide,
    rows,
):
    blocks = conf_ref.shape[0]
    widen(patch_ref, wide)
    spread_weights(conf_ref, weight_wide)

    def copy(b, state):
        rows[pl.ds(pl.multiple_of(b * LANES, LANES), LANES), :] = rows_ref[b]
        return state

    lax.fori_loop(0, blocks, copy, 0)

    def renew(o, state):
        def put(k):
            rows[pl.ds(place_ref[o, k], 1), :] = wide[pl.ds(o * SLOT + k, 1), :]

        for k in range(EAGER):
            put(k)

        @pl.when(place_ref[o, PAD - 2] > EAGER)
        def _():
            for k in range(EAGER, PATCH):
                put(k)

        count = place_ref[o, PAD - 1]

        @pl.when(count > PATCH)
        def _():
            pltpu.sync_copy(more_ref.at[o], more_narrow)
            more_wide[...] = more_narrow[...].astype(jnp.float32)

            def put_more(k, inner):
                rows[pl.ds(place_ref[o, k], 1), :] = more_wide[pl.ds(k - PATCH, 1), :]
                return inner

            lax.fori_loop(PATCH, count, put_more, 0)

        return state

    lax.fori_loop(0, place_ref.shape[0], renew, 0)

    def build(g, state):
        first = g * TOGETHER
        start = pl.multiple_of(first * LANES, LANES)
        build_blocks(
            first,
            [rows[pl.ds(start + c * LANES, LANES), :] for c in range(TOGETHER)],
            count_ref,
            conf_ref,
            rating_ref,
            weight_wide,
            turned,
            weighted,
            inside,
            right,
        )
        return state

    lax.fori_loop(0, blocks // TOGETHER, build, 0)


def build_items(places, counts, rows, patch, more, confidence, rating):
    blocks = confidence.shape[0]
    vmem = pl.BlockSpec(memory_space=pltpu.VMEM)
    smem = pl.BlockSpec(memory_space=pltpu.SMEM)
    matrices = pltpu.VMEM((blocks, LANES, LANES), jnp.bfloat16)
    vectors = pltpu.VMEM((blocks, 8, LANES), jnp.float32)
    return pl.pallas_call(
        build_items_kernel,
        in_specs=[smem] * 2 + [vmem] * 2 + [pl.BlockSpec(memory_space=pl.ANY)] + [vmem] * 2,
        out_specs=[vmem] * 4,
        out_shape=[matrices, matrices, vectors, vectors],
        scratch_shapes=[
            pltpu.VMEM(patch.shape, jnp.float32),
            pltpu.VMEM(more.shape[1:], jnp.bfloat16),
            pltpu.VMEM(more.shape[1:], jnp.float32),
            pltpu.VMEM((blocks, LANES, LANES), jnp.float32),
            pltpu.VMEM((blocks * LANES + 8, LANES), jnp.float32),
        ],
        compiler_params=pltpu.CompilerParams(vmem_limit_bytes=48 << 20),
        name="build_items",
    )(places, counts, rows, patch, more, confidence, rating)


def solve_items_kernel(
    gram_scale,
    turned,
    weighted,
    inside,
    right,
    warm_ref,
    gram_ref,
    table_ref,
    out_ref,
    x_ref,
    r_ref,
    p_ref,
    g_ref,
    solved,
    sems,
):
    batch = solved.shape[0]
    rest = pl.ds(batch, table_ref.shape[0] - batch)
    keep = pltpu.make_async_copy(table_ref.at[rest], out_ref.at[rest], sems.at[0])
    keep.start()
    start_from(warm_ref, x_ref, p_ref)
    r_ref[...] = right[...]
    conjugate(gram_ref[...] * gram_scale, turned, weighted, inside, x_ref, r_ref, p_ref, g_ref)
    give(x_ref, solved)
    put = pltpu.make_async_copy(solved, out_ref.at[pl.ds(0, batch)], sems.at[1])
    put.start()
    put.wait()
    keep.wait()


def solve_items(built, table, gram, gram_scale):
    blocks = built[0].shape[0]
    vmem = pl.BlockSpec(memory_space=pltpu.VMEM)
    hbm = pl.BlockSpec(memory_space=pltpu.HBM)
    return pl.pallas_call(
        functools.partial(solve_items_kernel, gram_scale),
        in_specs=[vmem] * 6 + [hbm],
        out_specs=hbm,
        out_shape=jax.ShapeDtypeStruct(table.shape, jnp.float32),
        scratch_shapes=[pltpu.VMEM((blocks, 8, LANES), jnp.float32)] * 4
        + [pltpu.VMEM((4 * blocks, LANES), jnp.float32), pltpu.SemaphoreType.DMA((2,))],
        compiler_params=pltpu.CompilerParams(vmem_limit_bytes=32 << 20),
        name="solve_items",
    )(*built, table[: 4 * blocks], gram, table)


def exchange(values):
    return lax.all_to_all(values, AXES, split_axis=0, concat_axis=0, tiled=True)


def local_gram(table):
    return jnp.dot(
        table.T, table, precision=lax.Precision.HIGH, preferred_element_type=jnp.float32
    )


def shards(
    user_table,
    item_table,
    item_owner,
    item_row,
    user_confidence,
    user_rating,
    user_counts,
    user_owner,
    user_row,
    item_confidence,
    item_rating,
    item_counts,
):
    devices = lax.axis_size(AXES)
    tab_rows, width = user_table.shape
    blocks = user_counts.shape[0]
    batch = blocks * user_counts.shape[1]
    gram_scale = global_weight / (tab_rows * devices)

    def by_block(values):
        return values.reshape(blocks, -1)

    requests, item_slots, user_slots, places = bucket(
        by_block(item_owner),
        by_block(item_row),
        by_block(user_owner),
        by_block(user_row),
        local_gram(item_table),
        batch,
    )
    came = exchange(requests[:, None, :])[:, 0]
    wanted = came[:, :width].astype(jnp.int32)
    gram_row = jnp.sum(came[:, width:], 0, keepdims=True)
    most = jnp.max(wanted[:, -1])
    fresh = jnp.minimum(wanted[:, PAD : 2 * PAD], batch - 1)

    replies = exchange(gather(0, CAP, PAD, wanted, item_table, gram_row))
    early = gather(PAD + PATCH, CAP - PATCH, EARLY, wanted, user_table)
    still = local_gram(user_table[batch:])
    early, still, replies = lax.optimization_barrier((early, still, replies))
    early = exchange(early)
    renewed, patch = solve_users(
        item_slots,
        wanted,
        user_counts,
        replies.reshape(-1, width),
        by_block(user_confidence),
        by_block(user_rating),
        user_table,
        still,
        gram_scale,
    )
    new_users = jnp.concatenate([renewed, user_table[batch:]], 0)

    patch, early = lax.optimization_barrier((patch, early))
    patch = exchange(patch)
    narrow = renewed.astype(jnp.bfloat16)

    def another(state):
        done, kept = state
        rows = narrow[lax.dynamic_slice_in_dim(fresh, done, SLOT, 1)]
        return done + SLOT, lax.dynamic_update_slice(kept, exchange(rows), (0, done - PATCH, 0))

    _, more = lax.while_loop(lambda state: state[0] < most, another, (jnp.int32(PATCH), replies))
    rows = unsort(user_slots, early.reshape(-1, width))
    patch, rows = lax.optimization_barrier((patch, rows))
    gram_row = jnp.sum(patch[:, PATCH:].astype(jnp.float32), (0, 1))
    user_gram = exchange(jnp.broadcast_to(gram_row[None, None], (devices, 1, width)))[:, 0]
    built = build_items(
        places,
        item_counts,
        rows,
        patch.reshape(-1, width),
        more,
        by_block(item_confidence),
        by_block(item_rating),
    )
    return (new_users, solve_items(built, item_table, user_gram, gram_scale))


def solution(mesh):
    spec = P(AXES, None)
    flat = P(AXES)
    in_specs = (spec, spec, spec, flat, flat, flat, spec, spec, flat, flat, flat, spec)
    return jax.shard_map(
        shards, mesh=mesh, in_specs=in_specs, out_specs=(spec, spec), check_vma=False
    )
```

```python
import functools

import jax
import jax.numpy as jnp
from jax import lax
from jax.experimental import pallas as pl
from jax.experimental.pallas import tpu as pltpu
from jax.sharding import PartitionSpec as P

ITERS = 8
AXES = ("gx", "gy")
LIVE = 112
PAD = 64
CAP = 60
PATCH = 14
SLOT = 16
EARLY = 48
EAGER = 6
TOGETHER = 4
LANES = 128

ridge_weight = 1.0
global_weight = 256.0
guard_eps = 1e-06


def bucket_kernel(batch, *refs):
    inputs, (request_ref, slot0, slot1, place_ref) = refs[:5], refs[5:9]
    copies = [
        pltpu.make_async_copy(source, target, refs[14].at[k])
        for k, (source, target) in enumerate(zip(inputs, refs[9:14]))
    ]
    owner0, row0, owner1, row1, table_ref = refs[9:14]
    for copy in copies:
        copy.start()
    for copy in copies:
        copy.wait()

    chunks = owner0.shape[0]
    sub = lax.broadcasted_iota(jnp.int32, (LANES, LANES), 0)
    lane = lax.broadcasted_iota(jnp.int32, (LANES, LANES), 1)
    below = jnp.where(sub < lane, 1.0, 0.0)
    prefix = jnp.concatenate([below, jnp.ones_like(below)], 1).astype(jnp.bfloat16)
    place = sub % PAD
    first_half = sub < PAD
    group = 16
    zero = jnp.zeros((LANES, LANES), jnp.float32)
    wide = jnp.concatenate([zero, zero], 1)
    steps = chunks // group
    shares = [table_ref.shape[0] * part // (16 * steps) for part in (9, 6)]

    def add_gram(total, start, count):
        rows = table_ref[pl.ds(pl.multiple_of(start, LANES), count), :]
        head = rows.astype(jnp.bfloat16)
        rest = (rows - head.astype(jnp.float32)).astype(jnp.bfloat16)
        return total + jnp.dot(
            rows.T.astype(jnp.bfloat16),
            jnp.concatenate([head, rest], 1),
            preferred_element_type=jnp.float32,
        )

    def step(half, g, state):
        carry, wanted, gram = state
        gram = add_gram(gram, half * steps * shares[0] + g * shares[half], shares[half])
        start = pl.multiple_of(g * group, group)
        owners = (owner0, owner1)[half][pl.ds(start, group), :]
        rows = (row0, row1)[half][pl.ds(start, group), :]
        position = lax.broadcasted_iota(jnp.int32, owners.shape, 1)
        masked = jnp.where(position < LIVE, owners, -1)
        unit = jnp.where(rows < batch, 1.0, float(PAD)) if half == 1 else None
        hot = []
        counted = []
        for c in range(group):
            hit = sub == masked[c : c + 1, :]
            hot.append(jnp.where(hit, 1.0, 0.0))
            tally = hot[c] if half == 0 else jnp.where(hit, unit[c : c + 1, :], 0.0)
            counted.append(
                jnp.dot(tally.astype(jnp.bfloat16), prefix, preferred_element_type=jnp.float32)
            )
        ranks = []
        for c in range(group):
            before = counted[c][:, :LANES] + carry
            ranks.append(jnp.sum(before * hot[c], 0, keepdims=True).astype(jnp.int32))
            carry = carry + counted[c][:, LANES:]
        ranks = jnp.concatenate(ranks, 0)
        if half == 1:
            ranks = jnp.where(rows < batch, ranks % PAD, CAP - 1 - ranks // PAD)
        high = (rows // PAD).astype(jnp.float32)
        low = (rows % PAD).astype(jnp.float32)
        if half == 1:
            high, low = low, high
        lane_row = position.astype(jnp.float32)
        puts = []
        for c in range(group):
            chosen = place == ranks[c : c + 1, :]
            value = jnp.where(first_half, high[c : c + 1, :], low[c : c + 1, :])
            put = jnp.where(chosen, value, 0.0).astype(jnp.bfloat16)
            if half == 1:
                spot = jnp.where(
                    first_half, lane_row[c : c + 1, :], (g * group + c).astype(jnp.float32)
                )
                put = jnp.concatenate(
                    [put, jnp.where(chosen, spot, 0.0).astype(jnp.bfloat16)], 0
                )
            puts.append(put)
        wanted = wanted + lax.dot_general(
            jnp.concatenate(hot, 1).astype(jnp.bfloat16),
            jnp.concatenate(puts, 1),
            (((1,), (1,)), ((), ())),
            preferred_element_type=jnp.float32,
        )
        if half == 0:
            slot0[pl.ds(start, group), :] = owners * PAD + ranks
        else:
            slot1[pl.ds(start, group), :] = owners * EARLY + jnp.where(
                ranks < PATCH, EARLY - 1, ranks - PATCH
            )
        return carry, wanted, gram

    _, first, gram = lax.fori_loop(0, steps, functools.partial(step, 0), (zero, zero, wide))
    tally, second, gram = lax.fori_loop(0, steps, functools.partial(step, 1), (zero, wide, gram))
    done = steps * sum(shares)
    gram = add_gram(gram, done, table_ref.shape[0] - done)
    cross = gram[:, LANES:]
    spots = second[:, LANES:]
    second = second[:, :LANES]
    first = first * PAD + pltpu.roll(first, PAD, 1)
    second = second * PAD + pltpu.roll(second, PAD, 1)
    spots = spots + pltpu.roll(spots, PAD, 1) * LANES
    renewed = tally.astype(jnp.int32) % PAD
    most = jnp.max(renewed).astype(jnp.float32)
    request = jnp.where(lane < PAD, first, second)
    request_ref[:, :LANES] = jnp.where(lane == LANES - 1, most, request)
    request_ref[:, LANES:] = gram[:, :LANES] + cross + cross.T
    others = tally.astype(jnp.int32) // PAD
    used = (lane < renewed) | (lane >= CAP - others)
    places = jnp.where(used, spots.astype(jnp.int32), chunks * LANES)
    looked = jnp.where(others > CAP - PATCH, PATCH, jnp.minimum(renewed, PATCH))
    places = jnp.where(lane == PAD - 2, looked, places)
    place_ref[...] = jnp.where(lane == PAD - 1, renewed, places)


def bucket(owner0, row0, owner1, row1, table, batch):
    slots = jax.ShapeDtypeStruct(owner0.shape, jnp.int32)
    inputs = (owner0, row0, owner1, row1, table)
    return pl.pallas_call(
        functools.partial(bucket_kernel, batch),
        in_specs=[pl.BlockSpec(memory_space=pltpu.HBM)] * 5,
        out_shape=(
            jax.ShapeDtypeStruct((LANES, 2 * LANES), jnp.float32),
            slots,
            slots,
            jax.ShapeDtypeStruct((LANES, LANES), jnp.int32),
        ),
        scratch_shapes=[pltpu.VMEM(x.shape, x.dtype) for x in inputs]
        + [pltpu.SemaphoreType.DMA((5,))],
        compiler_params=pltpu.CompilerParams(vmem_limit_bytes=32 << 20),
        name="bucket",
    )(*[hold(x) for x in inputs])


def gather_kernel(first, count, per_step, request_ref, table_ref, *refs):
    out_ref, wide = refs[-2:]
    base = pl.program_id(0) * per_step
    depth = wide.shape[1]
    last = jnp.zeros((depth - count, LANES), jnp.float32)
    if len(refs) == 3:
        row = refs[0][...]
        head = row.astype(jnp.bfloat16).astype(jnp.float32)
        last = jnp.concatenate([head, row - head, last[2:]], 0)
    for k in range(2):
        wide[k, count:, :] = last

    def one(s, state):
        buffer = wide.at[s % 2]
        for i in range(count):
            index = request_ref[base + s, first + i]
            buffer[pl.ds(i, 1), :] = table_ref[pl.ds(index, 1), :]
        out_ref[s] = buffer[...].astype(jnp.bfloat16)
        return state

    lax.fori_loop(0, per_step, one, 0)


def gather(first, count, depth, requests, table, extra=None):
    devices = requests.shape[0]
    steps = 8
    per_step = devices // steps
    more = () if extra is None else (extra,)
    return pl.pallas_call(
        functools.partial(gather_kernel, first, count, per_step),
        grid=(steps,),
        in_specs=[
            pl.BlockSpec(memory_space=pltpu.SMEM),
            pl.BlockSpec(table.shape, lambda i: (0, 0)),
        ]
        + [pl.BlockSpec(extra.shape, lambda i: (0, 0)) for extra in more],
        out_specs=pl.BlockSpec((per_step, depth, LANES), lambda i: (i, 0, 0)),
        out_shape=pltpu.HBM((devices, depth, LANES), jnp.bfloat16),
        scratch_shapes=[pltpu.VMEM((2, depth, LANES), jnp.float32)],
        compiler_params=pltpu.CompilerParams(vmem_limit_bytes=32 << 20),
        name="gather_rows",
    )(requests, table, *more)


def unsort_kernel(slot_ref, reply_ref, out_ref, wide):
    widen(reply_ref, wide)

    def one(b, state):
        for t in range(LIVE):
            out_ref[b, pl.ds(t, 1), :] = wide[pl.ds(slot_ref[b, t], 1), :]
        out_ref[b, LIVE:, :] = jnp.zeros((LANES - LIVE, LANES), jnp.float32)
        return state

    lax.fori_loop(0, out_ref.shape[0], one, 0)


def unsort(slots, replies):
    blocks = slots.shape[0]
    return pl.pallas_call(
        unsort_kernel,
        in_specs=[pl.BlockSpec(memory_space=pltpu.SMEM), pl.BlockSpec(memory_space=pltpu.VMEM)],
        out_specs=pl.BlockSpec(memory_space=pltpu.VMEM),
        out_shape=pltpu.HBM((blocks, LANES, LANES), jnp.float32),
        scratch_shapes=[pltpu.VMEM(replies.shape, jnp.float32)],
        compiler_params=pltpu.CompilerParams(vmem_limit_bytes=32 << 20),
        name="unsort_rows",
    )(slots, replies)


def fold(value):
    return value + pltpu.roll(value, 4, 0)


def split(value):
    top = lax.broadcasted_iota(jnp.int32, value.shape, 0) < 4
    head = value.astype(jnp.bfloat16).astype(jnp.float32)
    return jnp.where(top, head, value - head).astype(jnp.bfloat16)


def widen(source, target):
    step = 512

    def one(i, state):
        start = pl.multiple_of(i * step, step)
        target[pl.ds(start, step), :] = source[pl.ds(start, step), :].astype(jnp.float32)
        return state

    lax.fori_loop(0, source.shape[0] // step, one, 0)


def spread_weights(conf_ref, weight_wide):
    blocks = conf_ref.shape[0]
    conf_turned = jnp.concatenate(
        [conf_ref[...], jnp.zeros((LANES - blocks, LANES), jnp.float32)], 0
    ).T
    for b in range(blocks):
        weight_wide[b] = jnp.broadcast_to(conf_turned[:, b : b + 1], (LANES, LANES))


def build_blocks(
    first, rows, count_ref, conf_ref, rating_ref, weight_wide, turned, weighted, inside, right, base=None
):
    base = first if base is None else base
    sub = lax.broadcasted_iota(jnp.int32, (8, LANES), 0)
    lane = lax.broadcasted_iota(jnp.int32, (8, LANES), 1)
    which = sub % 4
    sums = []
    for c, fetched in enumerate(rows):
        b = first + c
        pair, side = base // 2 + c // 2, pl.ds(c % 2 * LANES, LANES)
        turned[pair, :, side] = fetched.T.astype(jnp.bfloat16)
        weighted[pair, side, :] = (weight_wide[b] * fetched).astype(jnp.bfloat16)
        end0 = count_ref[b, 0]
        end1 = end0 + count_ref[b, 1]
        end2 = end1 + count_ref[b, 2]
        end3 = end2 + count_ref[b, 3]
        begin = jnp.where(which < 2, jnp.where(which == 0, 0, end0), jnp.where(which == 2, end1, end2))
        end = jnp.where(which < 2, jnp.where(which == 0, end0, end1), jnp.where(which == 2, end2, end3))
        mask = jnp.where((lane >= begin) & (lane < end), 1.0, 0.0)
        inside[base + c] = mask
        target = conf_ref[pl.ds(b, 1), :] * rating_ref[pl.ds(b, 1), :] * mask
        sums.append(
            jnp.dot(split(target), fetched.astype(jnp.bfloat16), preferred_element_type=jnp.float32)
        )
    for c, part in enumerate(sums):
        right[base + c] = fold(part)


def start_from(warm_ref, x_ref, p_ref):
    for b in range(x_ref.shape[0]):
        warm = warm_ref[pl.ds(4 * b, 4), :]
        both = jnp.concatenate([warm, warm], 0)
        x_ref[b] = both
        p_ref[b] = both


def give(x_ref, out_ref):
    for b in range(x_ref.shape[0]):
        out_ref[pl.ds(4 * b, 4), :] = x_ref[b, :4, :]


def conjugate(gram, turned, weighted, inside, x_ref, r_ref, p_ref, g_ref):
    blocks = x_ref.shape[0]
    gram_head = gram.astype(jnp.bfloat16)
    gram_tail = (gram - gram_head.astype(jnp.float32)).astype(jnp.bfloat16)
    gram_both = jnp.concatenate([gram_head, gram_tail], 1)
    group = 24
    nought = jnp.zeros((8, LANES), jnp.bfloat16)

    def apply_system(g):
        ids = [g * group + c for c in range(group)]
        dirs = [p_ref[b] for b in ids]
        cut = [split(d) for d in dirs]
        shared = jnp.dot(jnp.concatenate(cut, 0), gram_both, preferred_element_type=jnp.float32)
        along = []
        for c in range(0, group, 2):
            out = jnp.dot(
                jnp.concatenate(cut[c : c + 2], 0),
                turned[ids[c] // 2],
                preferred_element_type=jnp.float32,
            )
            along += [fold(out[:8, :LANES]), fold(out[8:, LANES:])]
        back = []
        for c in range(0, group, 2):
            one, two = [split(along[k] * inside[ids[k]]) for k in (c, c + 1)]
            both = jnp.concatenate(
                [jnp.concatenate([one, nought], 1), jnp.concatenate([nought, two], 1)], 0
            )
            out = jnp.dot(both, weighted[ids[c] // 2], preferred_element_type=jnp.float32)
            back += [out[:8], out[8:]]
        images = []
        for c in range(group):
            part = shared[8 * c : 8 * c + 8]
            images.append(
                fold(back[c] + part[:, :LANES] + part[:, LANES:]) + ridge_weight * dirs[c]
            )
        return ids, dirs, images

    for g in range(blocks // group):
        ids, dirs, images = apply_system(g)
        for c in range(group):
            resid = r_ref[ids[c]] - images[c]
            r_ref[ids[c]] = resid
            p_ref[ids[c]] = resid
            g_ref[ids[c]] = jnp.broadcast_to(
                jnp.sum(resid * resid, -1, keepdims=True), (8, LANES)
            )

    def iterate(i, state):
        for g in range(blocks // group):
            ids, dirs, images = apply_system(g)
            for c in range(group):
                b = ids[c]
                norm_now = g_ref[b]
                step_size = norm_now / (
                    jnp.sum(dirs[c] * images[c], -1, keepdims=True) + guard_eps
                )
                x_ref[b] = x_ref[b] + step_size * dirs[c]
                resid = r_ref[b] - step_size * images[c]
                r_ref[b] = resid
                norm_next = jnp.sum(resid * resid, -1, keepdims=True)
                p_ref[b] = resid + norm_next / (norm_now + guard_eps) * dirs[c]
                g_ref[b] = jnp.broadcast_to(norm_next, (8, LANES))
        return state

    lax.fori_loop(0, ITERS, iterate, 0)


def solve_users_kernel(
    gram_scale,
    slot_ref,
    wanted_ref,
    count_ref,
    reply_ref,
    conf_ref,
    rating_ref,
    table_ref,
    still_ref,
    out_ref,
    patch_ref,
    narrow,
    wide,
    table,
    weight_wide,
    rows,
    turned,
    weighted,
    inside,
    x_ref,
    r_ref,
    p_ref,
    g_ref,
    sems,
):
    blocks = conf_ref.shape[0]
    batch = 4 * blocks
    parts = 4
    depth = reply_ref.shape[0] // parts
    fetches = []
    for k in range(parts):
        part = pl.ds(k * depth, depth)
        fetches.append(pltpu.make_async_copy(reply_ref.at[part], narrow.at[part], sems.at[k]))
        fetches[k].start()
    load = pltpu.make_async_copy(table_ref, table, sems.at[parts])
    load.start()
    rest = pl.ds(batch, table_ref.shape[0] - batch)
    keep = pltpu.make_async_copy(table.at[rest], out_ref.at[rest], sems.at[parts + 1])
    spread_weights(conf_ref, weight_wide)
    rows[...] = jnp.zeros_like(rows)
    for k in range(parts):
        part = pl.ds(k * depth, depth)
        fetches[k].wait()
        widen(narrow.at[part], wide.at[part])

    def build(g, state):
        first = g * TOGETHER
        for c in range(TOGETHER):
            for t in range(LIVE):
                rows[c, pl.ds(t, 1), :] = wide[pl.ds(slot_ref[first + c, t], 1), :]
        build_blocks(
            first,
            [rows[c] for c in range(TOGETHER)],
            count_ref,
            conf_ref,
            rating_ref,
            weight_wide,
            turned,
            weighted,
            inside,
            r_ref,
        )
        return state

    lax.fori_loop(0, blocks // TOGETHER, build, 0)
    load.wait()
    keep.start()
    start_from(table, x_ref, p_ref)
    gram = wide[pl.ds(CAP, LANES, stride=PAD), :] + wide[pl.ds(CAP + 1, LANES, stride=PAD), :]
    conjugate(gram * gram_scale, turned, weighted, inside, x_ref, r_ref, p_ref, g_ref)
    give(x_ref, table)
    put = pltpu.make_async_copy(
        table.at[pl.ds(0, batch)], out_ref.at[pl.ds(0, batch)], sems.at[parts + 2]
    )
    put.start()

    solved = table[pl.ds(0, batch), :]
    head = solved.astype(jnp.bfloat16)
    rest = (solved - head.astype(jnp.float32)).astype(jnp.bfloat16)
    head_turned = head.astype(jnp.float32).T.astype(jnp.bfloat16)
    cross = jnp.dot(head_turned, rest, preferred_element_type=jnp.float32)
    gram = jnp.dot(head_turned, head, preferred_element_type=jnp.float32) + cross + cross.T
    rows[0] = still_ref[...] + gram

    def one(o, state):
        buffer = rows.at[1, pl.ds(pl.multiple_of(o % 2 * SLOT, SLOT), SLOT)]
        for i in range(PATCH):
            buffer[pl.ds(i, 1), :] = table[pl.ds(wanted_ref[o, PAD + i], 1), :]
        share = rows[0, pl.ds(o, 1), :]
        top = share.astype(jnp.bfloat16).astype(jnp.float32)
        buffer[pl.ds(PATCH, 1), :] = top
        buffer[pl.ds(PATCH + 1, 1), :] = share - top
        patch_ref[o] = buffer[...].astype(jnp.bfloat16)
        return state

    lax.fori_loop(0, wanted_ref.shape[0], one, 0)
    put.wait()
    keep.wait()


def solve_users(slots, wanted, counts, replies, confidence, rating, table, still, gram_scale):
    blocks = confidence.shape[0]
    vmem = pl.BlockSpec(memory_space=pltpu.VMEM)
    smem = pl.BlockSpec(memory_space=pltpu.SMEM)
    hbm = pl.BlockSpec(memory_space=pltpu.HBM)
    return pl.pallas_call(
        functools.partial(solve_users_kernel, gram_scale),
        in_specs=[smem, smem, smem, hbm, vmem, vmem, hbm, vmem],
        out_specs=[hbm, vmem],
        out_shape=[
            jax.ShapeDtypeStruct(table.shape, jnp.float32),
            pltpu.HBM((wanted.shape[0], SLOT, LANES), jnp.bfloat16),
        ],
        scratch_shapes=[
            pltpu.VMEM(replies.shape, jnp.bfloat16),
            pltpu.VMEM(replies.shape, jnp.float32),
            pltpu.VMEM(table.shape, jnp.float32),
            pltpu.VMEM((blocks, LANES, LANES), jnp.float32),
            pltpu.VMEM((TOGETHER, LANES, LANES), jnp.float32),
        ]
        + matrices(blocks)
        + [pltpu.SemaphoreType.DMA((7,))],
        compiler_params=pltpu.CompilerParams(vmem_limit_bytes=48 << 20),
        name="solve_users",
    )(slots, wanted, counts, hold(replies), confidence, rating, hold(table), still)


def matrices(blocks):
    return [
        pltpu.VMEM((blocks // 2, LANES, 2 * LANES), jnp.bfloat16),
        pltpu.VMEM((blocks // 2, 2 * LANES, LANES), jnp.bfloat16),
    ] + [pltpu.VMEM((blocks, 8, LANES), jnp.float32)] * 5


def build_items_kernel(
    place_ref,
    count_ref,
    rows_ref,
    patch_ref,
    more_ref,
    conf_ref,
    rating_ref,
    turned,
    weighted,
    inside,
    right,
    wide,
    more_narrow,
    more_wide,
    weight_wide,
    rows,
    sem,
):
    def renew(o, state):
        def put(k):
            rows[pl.ds(place_ref[o, k], 1), :] = wide[pl.ds(o * SLOT + k, 1), :]

        for k in range(EAGER):
            put(k)

        @pl.when(place_ref[o, PAD - 2] > EAGER)
        def _():
            for k in range(EAGER, PATCH):
                put(k)

        count = place_ref[o, PAD - 1]

        @pl.when(count > PATCH)
        def _():
            pltpu.sync_copy(more_ref.at[o], more_narrow)
            more_wide[...] = more_narrow[...].astype(jnp.float32)

            def put_more(k, inner):
                rows[pl.ds(place_ref[o, k], 1), :] = more_wide[pl.ds(k - PATCH, 1), :]
                return inner

            lax.fori_loop(PATCH, count, put_more, 0)

        return state

    @pl.when(pl.program_id(0) == 0)
    def _():
        load = pltpu.make_async_copy(rows_ref, rows.at[pl.ds(0, rows_ref.shape[0])], sem)
        load.start()
        widen(patch_ref, wide)
        spread_weights(conf_ref, weight_wide)
        load.wait()
        lax.fori_loop(0, place_ref.shape[0], renew, 0)

    first = pl.program_id(0) * TOGETHER
    start = pl.multiple_of(first * LANES, LANES)
    build_blocks(
        first,
        [rows[pl.ds(start + c * LANES, LANES), :] for c in range(TOGETHER)],
        count_ref,
        conf_ref,
        rating_ref,
        weight_wide,
        turned,
        weighted,
        inside,
        right,
        0,
    )


def build_items(places, counts, rows, patch, more, confidence, rating):
    blocks = confidence.shape[0]
    vmem = pl.BlockSpec(memory_space=pltpu.VMEM)
    smem = pl.BlockSpec(memory_space=pltpu.SMEM)
    hbm = pl.BlockSpec(memory_space=pltpu.HBM)
    pairs = TOGETHER // 2
    shapes = [
        ((blocks // 2, LANES, 2 * LANES), jnp.bfloat16, pairs),
        ((blocks // 2, 2 * LANES, LANES), jnp.bfloat16, pairs),
        ((blocks, 8, LANES), jnp.float32, TOGETHER),
        ((blocks, 8, LANES), jnp.float32, TOGETHER),
    ]
    return pl.pallas_call(
        build_items_kernel,
        grid=(blocks // TOGETHER,),
        in_specs=[smem, smem, hbm, vmem, hbm, vmem, vmem],
        out_specs=[
            pl.BlockSpec((step,) + shape[1:], lambda i: (i, 0, 0)) for shape, _, step in shapes
        ],
        out_shape=[pltpu.HBM(shape, kind) for shape, kind, _ in shapes],
        scratch_shapes=[
            pltpu.VMEM(patch.shape, jnp.float32),
            pltpu.VMEM(more.shape[1:], jnp.bfloat16),
            pltpu.VMEM(more.shape[1:], jnp.float32),
            pltpu.VMEM((blocks, LANES, LANES), jnp.float32),
            pltpu.VMEM((blocks * LANES + 8, LANES), jnp.float32),
            pltpu.SemaphoreType.DMA,
        ],
        compiler_params=pltpu.CompilerParams(vmem_limit_bytes=48 << 20),
        name="build_items",
    )(places, counts, hold(rows), patch, hold(more), confidence, rating)


def solve_items_kernel(gram_scale, *refs):
    built, (gram_ref, table_ref, out_ref, table) = refs[:4], refs[4:8]
    turned, weighted, inside, x_ref, r_ref, p_ref, g_ref, sems = refs[8:]
    loads = [
        pltpu.make_async_copy(source, target, sems.at[k])
        for k, (source, target) in enumerate(zip(built, (turned, weighted, inside, r_ref)))
    ]
    for load in loads:
        load.start()
    loads.append(pltpu.make_async_copy(table_ref, table, sems.at[4]))
    loads[4].start()
    batch = 4 * x_ref.shape[0]
    rest = pl.ds(batch, table.shape[0] - batch)
    keep = pltpu.make_async_copy(table.at[rest], out_ref.at[rest], sems.at[5])
    for load in loads:
        load.wait()
    keep.start()
    start_from(table, x_ref, p_ref)
    conjugate(gram_ref[...] * gram_scale, turned, weighted, inside, x_ref, r_ref, p_ref, g_ref)
    give(x_ref, table)
    first = pl.ds(0, batch)
    put = pltpu.make_async_copy(table.at[first], out_ref.at[first], sems.at[6])
    put.start()
    put.wait()
    keep.wait()


def solve_items(built, table, gram, gram_scale):
    blocks = built[2].shape[0]
    vmem = pl.BlockSpec(memory_space=pltpu.VMEM)
    hbm = pl.BlockSpec(memory_space=pltpu.HBM)
    return pl.pallas_call(
        functools.partial(solve_items_kernel, gram_scale),
        in_specs=[hbm] * 4 + [vmem, hbm],
        out_specs=hbm,
        out_shape=jax.ShapeDtypeStruct(table.shape, jnp.float32),
        scratch_shapes=[pltpu.VMEM(table.shape, jnp.float32)]
        + matrices(blocks)
        + [pltpu.SemaphoreType.DMA((7,))],
        compiler_params=pltpu.CompilerParams(vmem_limit_bytes=48 << 20),
        name="solve_items",
    )(*[hold(x) for x in built], gram, hold(table))


def hold(values):
    return pltpu.with_memory_space_constraint(values, pltpu.HBM)


def exchange(values):
    return lax.all_to_all(values, AXES, split_axis=0, concat_axis=0, tiled=True)


def local_gram(table):
    return jnp.dot(
        table.T, table, precision=lax.Precision.HIGH, preferred_element_type=jnp.float32
    )


def shards(
    user_table,
    item_table,
    item_owner,
    item_row,
    user_confidence,
    user_rating,
    user_counts,
    user_owner,
    user_row,
    item_confidence,
    item_rating,
    item_counts,
):
    devices = lax.axis_size(AXES)
    tab_rows, width = user_table.shape
    blocks = user_counts.shape[0]
    batch = blocks * user_counts.shape[1]
    gram_scale = global_weight / (tab_rows * devices)

    def by_block(values):
        return values.reshape(blocks, -1)

    requests, item_slots, user_slots, places = bucket(
        by_block(item_owner),
        by_block(item_row),
        by_block(user_owner),
        by_block(user_row),
        item_table,
        batch,
    )
    came = exchange(requests[:, None, :])[:, 0]
    wanted = came[:, :width].astype(jnp.int32)
    gram_row = jnp.sum(came[:, width:], 0, keepdims=True)
    most = jnp.max(wanted[:, -1])
    fresh = jnp.minimum(wanted[:, PAD : 2 * PAD], batch - 1)

    replies = exchange(gather(0, CAP, PAD, wanted, item_table, gram_row))
    early = gather(PAD + PATCH, CAP - PATCH, EARLY, wanted, user_table)
    still = local_gram(user_table[batch:])
    early, still, replies = lax.optimization_barrier((early, still, replies))
    early = exchange(early)
    new_users, patch = solve_users(
        item_slots,
        wanted,
        user_counts,
        replies.reshape(-1, width),
        by_block(user_confidence),
        by_block(user_rating),
        user_table,
        still,
        gram_scale,
    )
    patch, early = lax.optimization_barrier((patch, early))
    patch = exchange(patch)

    def another(state):
        done, kept = state
        narrow = new_users[:batch].astype(jnp.bfloat16)
        rows = narrow[lax.dynamic_slice_in_dim(fresh, done, SLOT, 1)]
        return done + SLOT, lax.dynamic_update_slice(kept, exchange(rows), (0, done - PATCH, 0))

    _, more = lax.while_loop(lambda state: state[0] < most, another, (jnp.int32(PATCH), replies))
    rows = unsort(user_slots, early.reshape(-1, width))
    patch, rows = lax.optimization_barrier((patch, rows))
    gram_row = jnp.sum(patch[:, PATCH:].astype(jnp.float32), (0, 1))
    user_gram = exchange(jnp.broadcast_to(gram_row[None, None], (devices, 1, width)))[:, 0]
    built = build_items(
        places,
        item_counts,
        rows.reshape(-1, width),
        patch.reshape(-1, width),
        more,
        by_block(item_confidence),
        by_block(item_rating),
    )
    return (new_users, solve_items(built, item_table, user_gram, gram_scale))


def solution(mesh):
    spec = P(AXES, None)
    flat = P(AXES)
    in_specs = (spec, spec, spec, flat, flat, flat, spec, spec, flat, flat, flat, spec)
    return jax.shard_map(
        shards, mesh=mesh, in_specs=in_specs, out_specs=(spec, spec), check_vma=False
    )
```

```python
import functools

import jax
import jax.numpy as jnp
from jax import lax
from jax.experimental import pallas as pl
from jax.experimental.pallas import tpu as pltpu
from jax.sharding import PartitionSpec as P

ITERS = 8
AXES = ("gx", "gy")
LIVE = 112
PAD = 64
CAP = 60
PATCH = 14
SLOT = 16
EARLY = 48
TOGETHER = 4
STRIDE = 12
LANES = 128

ridge_weight = 1.0
global_weight = 256.0
guard_eps = 1e-06


def bucket_kernel(batch, *refs):
    inputs, (request_ref, slot0, slot1, place_ref) = refs[:5], refs[5:9]
    copies = [
        pltpu.make_async_copy(source, target, refs[14].at[k])
        for k, (source, target) in enumerate(zip(inputs, refs[9:14]))
    ]
    owner0, row0, owner1, row1, table_ref = refs[9:14]
    for copy in copies:
        copy.start()
    for copy in copies:
        copy.wait()

    chunks = owner0.shape[0]
    sub = lax.broadcasted_iota(jnp.int32, (LANES, LANES), 0)
    lane = lax.broadcasted_iota(jnp.int32, (LANES, LANES), 1)
    below = jnp.where(sub < lane, 1.0, 0.0)
    prefix = jnp.concatenate([below, jnp.ones_like(below)], 1).astype(jnp.bfloat16)
    place = sub % PAD
    first_half = sub < PAD
    group = 24
    zero = jnp.zeros((LANES, LANES), jnp.float32)
    wide = jnp.concatenate([zero, zero], 1)
    steps = chunks // group
    shares = [table_ref.shape[0] * part // (16 * steps) for part in (9, 6)]

    def add_gram(total, start, count):
        rows = table_ref[pl.ds(pl.multiple_of(start, LANES), count), :]
        head = rows.astype(jnp.bfloat16)
        rest = (rows - head.astype(jnp.float32)).astype(jnp.bfloat16)
        return total + jnp.dot(
            rows.T.astype(jnp.bfloat16),
            jnp.concatenate([head, rest], 1),
            preferred_element_type=jnp.float32,
        )

    def step(half, g, state):
        carry, wanted, gram = state
        gram = add_gram(gram, half * steps * shares[0] + g * shares[half], shares[half])
        start = pl.multiple_of(g * group, group)
        owners = (owner0, owner1)[half][pl.ds(start, group), :]
        rows = (row0, row1)[half][pl.ds(start, group), :]
        position = lax.broadcasted_iota(jnp.int32, owners.shape, 1)
        masked = jnp.where(position < LIVE, owners, -1)
        unit = jnp.where(rows < batch, 1.0, float(PAD)) if half == 1 else None
        hot = []
        counted = []
        for c in range(group):
            hit = sub == masked[c : c + 1, :]
            hot.append(jnp.where(hit, 1.0, 0.0))
            tally = hot[c] if half == 0 else jnp.where(hit, unit[c : c + 1, :], 0.0)
            counted.append(
                jnp.dot(tally.astype(jnp.bfloat16), prefix, preferred_element_type=jnp.float32)
            )
        ranks = []
        for c in range(group):
            before = counted[c][:, :LANES] + carry
            ranks.append(jnp.sum(before * hot[c], 0, keepdims=True).astype(jnp.int32))
            carry = carry + counted[c][:, LANES:]
        ranks = jnp.concatenate(ranks, 0)
        if half == 1:
            ranks = jnp.where(rows < batch, ranks % PAD, CAP - 1 - ranks // PAD)
        high = (rows // PAD).astype(jnp.float32)
        low = (rows % PAD).astype(jnp.float32)
        if half == 1:
            high, low = low, high
        lane_row = position.astype(jnp.float32)
        puts = []
        for c in range(group):
            chosen = place == ranks[c : c + 1, :]
            value = jnp.where(first_half, high[c : c + 1, :], low[c : c + 1, :])
            put = jnp.where(chosen, value, 0.0).astype(jnp.bfloat16)
            if half == 1:
                spot = jnp.where(
                    first_half, lane_row[c : c + 1, :], (g * group + c).astype(jnp.float32)
                )
                put = jnp.concatenate(
                    [put, jnp.where(chosen, spot, 0.0).astype(jnp.bfloat16)], 0
                )
            puts.append(put)
        wanted = wanted + lax.dot_general(
            jnp.concatenate(hot, 1).astype(jnp.bfloat16),
            jnp.concatenate(puts, 1),
            (((1,), (1,)), ((), ())),
            preferred_element_type=jnp.float32,
        )
        if half == 0:
            slot0[pl.ds(start, group), :] = owners * PAD + ranks
        else:
            slot1[pl.ds(start, group), :] = owners * EARLY + jnp.where(
                ranks < PATCH, EARLY - 1, ranks - PATCH
            )
        return carry, wanted, gram

    _, first, gram = lax.fori_loop(0, steps, functools.partial(step, 0), (zero, zero, wide))
    tally, second, gram = lax.fori_loop(0, steps, functools.partial(step, 1), (zero, wide, gram))
    done = steps * sum(shares)
    gram = add_gram(gram, done, table_ref.shape[0] - done)
    cross = gram[:, LANES:]
    spots = second[:, LANES:]
    second = second[:, :LANES]
    first = first * PAD + pltpu.roll(first, PAD, 1)
    second = second * PAD + pltpu.roll(second, PAD, 1)
    spots = spots + pltpu.roll(spots, PAD, 1) * LANES
    renewed = tally.astype(jnp.int32) % PAD
    most = jnp.max(renewed).astype(jnp.float32)
    request = jnp.where(lane < PAD, first, second)
    request_ref[:, :LANES] = jnp.where(lane == LANES - 1, most, request)
    request_ref[:, LANES:] = gram[:, :LANES] + cross + cross.T
    others = tally.astype(jnp.int32) // PAD
    used = (lane < renewed) | (lane >= CAP - others)
    places = jnp.where(used, spots.astype(jnp.int32), chunks * LANES)
    places = jnp.where(lane == PAD - 2, most.astype(jnp.int32), places)
    place_ref[...] = jnp.where(lane == PAD - 1, renewed, places)


def bucket(owner0, row0, owner1, row1, table, batch):
    slots = jax.ShapeDtypeStruct(owner0.shape, jnp.int32)
    inputs = (owner0, row0, owner1, row1, table)
    return pl.pallas_call(
        functools.partial(bucket_kernel, batch),
        in_specs=[pl.BlockSpec(memory_space=pltpu.HBM)] * 5,
        out_shape=(
            jax.ShapeDtypeStruct((LANES, 2 * LANES), jnp.float32),
            slots,
            slots,
            jax.ShapeDtypeStruct((LANES, LANES), jnp.int32),
        ),
        scratch_shapes=[pltpu.VMEM(x.shape, x.dtype) for x in inputs]
        + [pltpu.SemaphoreType.DMA((5,))],
        compiler_params=pltpu.CompilerParams(vmem_limit_bytes=32 << 20),
        name="bucket",
    )(*[hold(x) for x in inputs])


def gather_kernel(first, count, per_step, request_ref, table_ref, *refs):
    out_ref, wide = refs[-2:]
    base = pl.program_id(0) * per_step
    depth = wide.shape[1]
    last = jnp.zeros((depth - count, LANES), jnp.float32)
    if len(refs) == 3:
        row = refs[0][...]
        head = row.astype(jnp.bfloat16).astype(jnp.float32)
        last = jnp.concatenate([head, row - head, last[2:]], 0)
    for k in range(2):
        wide[k, count:, :] = last

    sub = lax.broadcasted_iota(jnp.int32, (8, LANES), 0)

    def one(s, state):
        buffer = wide.at[s % 2]
        for q in range(0, count, 8):
            part = None
            for i in range(min(8, count - q)):
                index = request_ref[base + s, first + q + i]
                row = jnp.broadcast_to(table_ref[pl.ds(index, 1), :], (8, LANES))
                part = row if part is None else jnp.where(sub == i, row, part)
            height = min(8, count - q)
            buffer[pl.ds(q, height), :] = part[:height]
        out_ref[s] = buffer[...].astype(jnp.bfloat16)
        return state

    lax.fori_loop(0, per_step, one, 0)


def gather(first, count, depth, requests, table, extra=None):
    devices = requests.shape[0]
    steps = 8
    per_step = devices // steps
    more = () if extra is None else (extra,)
    return pl.pallas_call(
        functools.partial(gather_kernel, first, count, per_step),
        grid=(steps,),
        in_specs=[
            pl.BlockSpec(memory_space=pltpu.SMEM),
            pl.BlockSpec(table.shape, lambda i: (0, 0)),
        ]
        + [pl.BlockSpec(extra.shape, lambda i: (0, 0)) for extra in more],
        out_specs=pl.BlockSpec((per_step, depth, LANES), lambda i: (i, 0, 0)),
        out_shape=pltpu.HBM((devices, depth, LANES), jnp.bfloat16),
        scratch_shapes=[pltpu.VMEM((2, depth, LANES), jnp.float32)],
        compiler_params=pltpu.CompilerParams(vmem_limit_bytes=32 << 20),
        name="gather_rows",
    )(requests, table, *more)


def unsort_kernel(slot_ref, reply_ref, out_ref, wide):
    widen(reply_ref, wide)

    def one(b, state):
        for t in range(LIVE):
            out_ref[b, pl.ds(t, 1), :] = wide[pl.ds(slot_ref[b, t], 1), :]
        out_ref[b, LIVE:, :] = jnp.zeros((LANES - LIVE, LANES), jnp.float32)
        return state

    lax.fori_loop(0, out_ref.shape[0], one, 0)


def unsort(slots, replies):
    blocks = slots.shape[0]
    return pl.pallas_call(
        unsort_kernel,
        in_specs=[pl.BlockSpec(memory_space=pltpu.SMEM), pl.BlockSpec(memory_space=pltpu.VMEM)],
        out_specs=pl.BlockSpec(memory_space=pltpu.VMEM),
        out_shape=pltpu.HBM((blocks, LANES, LANES), jnp.float32),
        scratch_shapes=[pltpu.VMEM(replies.shape, jnp.float32)],
        compiler_params=pltpu.CompilerParams(vmem_limit_bytes=32 << 20),
        name="unsort_rows",
    )(slots, replies)


def fold(value):
    return value + pltpu.roll(value, 4, 0)


def split(value):
    top = lax.broadcasted_iota(jnp.int32, value.shape, 0) < 4
    head = value.astype(jnp.bfloat16).astype(jnp.float32)
    return jnp.where(top, head, value - head).astype(jnp.bfloat16)


def widen(source, target):
    step = 512

    def one(i, state):
        start = pl.multiple_of(i * step, step)
        target[pl.ds(start, step), :] = source[pl.ds(start, step), :].astype(jnp.float32)
        return state

    lax.fori_loop(0, source.shape[0] // step, one, 0)


def spread_weights(conf_ref, weight_wide):
    blocks = conf_ref.shape[0]
    conf_turned = jnp.concatenate(
        [conf_ref[...], jnp.zeros((LANES - blocks, LANES), jnp.float32)], 0
    ).T
    for b in range(blocks):
        weight_wide[b] = jnp.broadcast_to(conf_turned[:, b : b + 1], (LANES, LANES))


def build_blocks(
    first, rows, count_ref, conf_ref, rating_ref, weight_wide, turned, weighted, inside, right, base=None
):
    base = first if base is None else base
    sub = lax.broadcasted_iota(jnp.int32, (8, LANES), 0)
    lane = lax.broadcasted_iota(jnp.int32, (8, LANES), 1)
    which = sub % 4
    sums = []
    for c, fetched in enumerate(rows):
        b = first + c
        pair, side = base // 2 + c // 2, pl.ds(c % 2 * LANES, LANES)
        turned[pair, :, side] = fetched.astype(jnp.bfloat16).T
        weighted[pair, side, :] = (weight_wide[b] * fetched).astype(jnp.bfloat16)
        end0 = count_ref[b, 0]
        end1 = end0 + count_ref[b, 1]
        end2 = end1 + count_ref[b, 2]
        end3 = end2 + count_ref[b, 3]
        begin = jnp.where(which < 2, jnp.where(which == 0, 0, end0), jnp.where(which == 2, end1, end2))
        end = jnp.where(which < 2, jnp.where(which == 0, end0, end1), jnp.where(which == 2, end2, end3))
        mask = jnp.where((lane >= begin) & (lane < end), 1.0, 0.0)
        inside[base + c] = mask
        target = conf_ref[pl.ds(b, 1), :] * rating_ref[pl.ds(b, 1), :] * mask
        sums.append(
            jnp.dot(split(target), fetched.astype(jnp.bfloat16), preferred_element_type=jnp.float32)
        )
    for c, part in enumerate(sums):
        right[base + c] = fold(part)


def start_from(warm_ref, x_ref, p_ref):
    for b in range(x_ref.shape[0]):
        warm = warm_ref[pl.ds(4 * b, 4), :]
        both = jnp.concatenate([warm, warm], 0)
        x_ref[b] = both
        p_ref[b] = both


def give(x_ref, out_ref):
    for b in range(x_ref.shape[0]):
        out_ref[pl.ds(4 * b, 4), :] = x_ref[b, :4, :]


def conjugate(gram, turned, weighted, inside, x_ref, r_ref, p_ref, g_ref, midway=None):
    blocks = x_ref.shape[0]
    gram_head = gram.astype(jnp.bfloat16)
    gram_tail = (gram - gram_head.astype(jnp.float32)).astype(jnp.bfloat16)
    gram_both = jnp.concatenate([gram_head, gram_tail], 1)
    group = 24
    nought = jnp.zeros((8, LANES), jnp.bfloat16)

    def apply_system(g):
        ids = [g * group + c for c in range(group)]
        dirs = [p_ref[b] for b in ids]
        cut = [split(d) for d in dirs]
        shared = jnp.dot(jnp.concatenate(cut, 0), gram_both, preferred_element_type=jnp.float32)
        along = []
        for c in range(0, group, 2):
            out = jnp.dot(
                jnp.concatenate(cut[c : c + 2], 0),
                turned[ids[c] // 2],
                preferred_element_type=jnp.float32,
            )
            along += [fold(out[:8, :LANES]), fold(out[8:, LANES:])]
        back = []
        for c in range(0, group, 2):
            one, two = [split(along[k] * inside[ids[k]]) for k in (c, c + 1)]
            both = jnp.concatenate(
                [jnp.concatenate([one, nought], 1), jnp.concatenate([nought, two], 1)], 0
            )
            out = jnp.dot(both, weighted[ids[c] // 2], preferred_element_type=jnp.float32)
            back += [out[:8], out[8:]]
        images = []
        for c in range(group):
            part = shared[8 * c : 8 * c + 8]
            images.append(
                fold(back[c] + part[:, :LANES] + part[:, LANES:]) + ridge_weight * dirs[c]
            )
        return ids, dirs, images

    for g in range(blocks // group):
        ids, dirs, images = apply_system(g)
        for c in range(group):
            resid = r_ref[ids[c]] - images[c]
            r_ref[ids[c]] = resid
            p_ref[ids[c]] = resid
            g_ref[ids[c]] = jnp.broadcast_to(
                jnp.sum(resid * resid, -1, keepdims=True), (8, LANES)
            )

    if midway is not None:
        midway()

    def iterate(i, state):
        for g in range(blocks // group):
            ids, dirs, images = apply_system(g)
            for c in range(group):
                b = ids[c]
                norm_now = g_ref[b]
                step_size = norm_now / (
                    jnp.sum(dirs[c] * images[c], -1, keepdims=True) + guard_eps
                )
                x_ref[b] = x_ref[b] + step_size * dirs[c]
                resid = r_ref[b] - step_size * images[c]
                r_ref[b] = resid
                norm_next = jnp.sum(resid * resid, -1, keepdims=True)
                p_ref[b] = resid + norm_next / (norm_now + guard_eps) * dirs[c]
                g_ref[b] = jnp.broadcast_to(norm_next, (8, LANES))
        return state

    lax.fori_loop(0, ITERS, iterate, 0)


def solve_users_kernel(
    gram_scale,
    slot_ref,
    wanted_ref,
    count_ref,
    reply_ref,
    conf_ref,
    rating_ref,
    table_ref,
    still_ref,
    out_ref,
    patch_ref,
    narrow,
    wide,
    table,
    weight_wide,
    rows,
    turned,
    weighted,
    inside,
    x_ref,
    r_ref,
    p_ref,
    g_ref,
    sems,
):
    blocks = conf_ref.shape[0]
    batch = 4 * blocks
    parts = 4
    depth = reply_ref.shape[0] // parts
    fetches = []
    for k in range(parts):
        part = pl.ds(k * depth, depth)
        fetches.append(pltpu.make_async_copy(reply_ref.at[part], narrow.at[part], sems.at[k]))
        fetches[k].start()
    load = pltpu.make_async_copy(table_ref, table, sems.at[parts])
    load.start()
    rest = pl.ds(batch, table_ref.shape[0] - batch)
    keep = pltpu.make_async_copy(table.at[rest], out_ref.at[rest], sems.at[parts + 1])
    spread_weights(conf_ref, weight_wide)
    rows[...] = jnp.zeros_like(rows)
    for k in range(parts):
        part = pl.ds(k * depth, depth)
        fetches[k].wait()
        widen(narrow.at[part], wide.at[part])

    def build(g, state):
        first = g * TOGETHER
        for c in range(TOGETHER):
            for t in range(LIVE):
                rows[c, pl.ds(t, 1), :] = wide[pl.ds(slot_ref[first + c, t], 1), :]
        build_blocks(
            first,
            [rows[c] for c in range(TOGETHER)],
            count_ref,
            conf_ref,
            rating_ref,
            weight_wide,
            turned,
            weighted,
            inside,
            r_ref,
        )
        return state

    lax.fori_loop(0, blocks // TOGETHER, build, 0)
    load.wait()
    keep.start()
    start_from(table, x_ref, p_ref)
    gram = wide[pl.ds(CAP, LANES, stride=PAD), :] + wide[pl.ds(CAP + 1, LANES, stride=PAD), :]
    conjugate(gram * gram_scale, turned, weighted, inside, x_ref, r_ref, p_ref, g_ref)
    give(x_ref, table)
    put = pltpu.make_async_copy(
        table.at[pl.ds(0, batch)], out_ref.at[pl.ds(0, batch)], sems.at[parts + 2]
    )
    put.start()

    solved = table[pl.ds(0, batch), :]
    head = solved.astype(jnp.bfloat16)
    rest = (solved - head.astype(jnp.float32)).astype(jnp.bfloat16)
    head_turned = head.astype(jnp.float32).T.astype(jnp.bfloat16)
    cross = jnp.dot(head_turned, rest, preferred_element_type=jnp.float32)
    gram = jnp.dot(head_turned, head, preferred_element_type=jnp.float32) + cross + cross.T
    rows[0] = still_ref[...] + gram

    def one(o, state):
        buffer = rows.at[1, pl.ds(pl.multiple_of(o % 2 * SLOT, SLOT), SLOT)]
        for i in range(PATCH):
            buffer[pl.ds(i, 1), :] = table[pl.ds(wanted_ref[o, PAD + i], 1), :]
        share = rows[0, pl.ds(o, 1), :]
        top = share.astype(jnp.bfloat16).astype(jnp.float32)
        buffer[pl.ds(PATCH, 1), :] = top
        buffer[pl.ds(PATCH + 1, 1), :] = share - top
        patch_ref[o] = buffer[...].astype(jnp.bfloat16)
        return state

    lax.fori_loop(0, wanted_ref.shape[0], one, 0)
    put.wait()
    keep.wait()


def solve_users(slots, wanted, counts, replies, confidence, rating, table, still, gram_scale):
    blocks = confidence.shape[0]
    vmem = pl.BlockSpec(memory_space=pltpu.VMEM)
    smem = pl.BlockSpec(memory_space=pltpu.SMEM)
    hbm = pl.BlockSpec(memory_space=pltpu.HBM)
    return pl.pallas_call(
        functools.partial(solve_users_kernel, gram_scale),
        in_specs=[smem, smem, smem, hbm, vmem, vmem, hbm, vmem],
        out_specs=[hbm, vmem],
        out_shape=[
            jax.ShapeDtypeStruct(table.shape, jnp.float32),
            pltpu.HBM((wanted.shape[0], SLOT, LANES), jnp.bfloat16),
        ],
        scratch_shapes=[
            pltpu.VMEM(replies.shape, jnp.bfloat16),
            pltpu.VMEM(replies.shape, jnp.float32),
            pltpu.VMEM(table.shape, jnp.float32),
            pltpu.VMEM((blocks, LANES, LANES), jnp.float32),
            pltpu.VMEM((TOGETHER, LANES, LANES), jnp.float32),
        ]
        + matrices(blocks)
        + [pltpu.SemaphoreType.DMA((7,))],
        compiler_params=pltpu.CompilerParams(vmem_limit_bytes=48 << 20),
        name="solve_users",
    )(slots, wanted, counts, hold(replies), confidence, rating, hold(table), still)


def matrices(blocks):
    return [
        pltpu.VMEM((blocks // 2, LANES, 2 * LANES), jnp.bfloat16),
        pltpu.VMEM((blocks // 2, 2 * LANES, LANES), jnp.bfloat16),
    ] + [pltpu.VMEM((blocks, 8, LANES), jnp.float32)] * 5


def build_items_kernel(
    place_ref,
    count_ref,
    rows_ref,
    patch_ref,
    more_ref,
    conf_ref,
    rating_ref,
    turned,
    weighted,
    inside,
    right,
    wide,
    more_narrow,
    more_wide,
    weight_wide,
    rows,
    sem,
):
    def renew(o, state):
        for k in range(PATCH):
            rows[pl.ds(place_ref[o, k], 1), :] = wide[pl.ds(o * SLOT + k, 1), :]
        return state

    def renew_more(o, state):
        count = place_ref[o, PAD - 1]

        @pl.when(count > PATCH)
        def _():
            pltpu.sync_copy(more_ref.at[o], more_narrow)
            more_wide[...] = more_narrow[...].astype(jnp.float32)

            def put(k, inner):
                rows[pl.ds(place_ref[o, k], 1), :] = more_wide[pl.ds(k - PATCH, 1), :]
                return inner

            lax.fori_loop(PATCH, count, put, 0)

        return state

    @pl.when(pl.program_id(0) == 0)
    def _():
        load = pltpu.make_async_copy(rows_ref, rows.at[pl.ds(0, rows_ref.shape[0])], sem)
        load.start()
        widen(patch_ref, wide)
        spread_weights(conf_ref, weight_wide)
        load.wait()
        lax.fori_loop(0, place_ref.shape[0], renew, 0, unroll=4)

        @pl.when(place_ref[0, PAD - 2] > PATCH)
        def _():
            lax.fori_loop(0, place_ref.shape[0], renew_more, 0)

    first = pl.program_id(0) * STRIDE
    start = pl.multiple_of(first * LANES, LANES)
    build_blocks(
        first,
        [rows[pl.ds(start + c * LANES, LANES), :] for c in range(STRIDE)],
        count_ref,
        conf_ref,
        rating_ref,
        weight_wide,
        turned,
        weighted,
        inside,
        right,
        0,
    )


def build_items(places, counts, rows, patch, more, confidence, rating):
    blocks = confidence.shape[0]
    vmem = pl.BlockSpec(memory_space=pltpu.VMEM)
    smem = pl.BlockSpec(memory_space=pltpu.SMEM)
    hbm = pl.BlockSpec(memory_space=pltpu.HBM)
    pairs = STRIDE // 2
    shapes = [
        ((blocks // 2, LANES, 2 * LANES), jnp.bfloat16, pairs),
        ((blocks // 2, 2 * LANES, LANES), jnp.bfloat16, pairs),
        ((blocks, 8, LANES), jnp.float32, STRIDE),
        ((blocks, 8, LANES), jnp.float32, STRIDE),
    ]
    return pl.pallas_call(
        build_items_kernel,
        grid=(blocks // STRIDE,),
        in_specs=[smem, smem, hbm, vmem, hbm, vmem, vmem],
        out_specs=[
            pl.BlockSpec((step,) + shape[1:], lambda i: (i, 0, 0)) for shape, _, step in shapes
        ],
        out_shape=[pltpu.HBM(shape, kind) for shape, kind, _ in shapes],
        scratch_shapes=[
            pltpu.VMEM(patch.shape, jnp.float32),
            pltpu.VMEM(more.shape[1:], jnp.bfloat16),
            pltpu.VMEM(more.shape[1:], jnp.float32),
            pltpu.VMEM((blocks, LANES, LANES), jnp.float32),
            pltpu.VMEM((blocks * LANES + 8, LANES), jnp.float32),
            pltpu.SemaphoreType.DMA,
        ],
        compiler_params=pltpu.CompilerParams(vmem_limit_bytes=48 << 20),
        name="build_items",
    )(places, counts, hold(rows), patch, hold(more), confidence, rating)


def solve_items_kernel(gram_scale, *refs):
    built, (warm_ref, gram_ref, table_ref, out_ref, table) = refs[:4], refs[4:9]
    turned, weighted, inside, x_ref, r_ref, p_ref, g_ref, sems = refs[9:]
    loads = [
        pltpu.make_async_copy(source, target, sems.at[k])
        for k, (source, target) in enumerate(zip(built, (turned, weighted, inside, r_ref)))
    ]
    for load in loads:
        load.start()
    batch = 4 * x_ref.shape[0]
    rest = pl.ds(batch, table.shape[0] - batch)
    fetch = pltpu.make_async_copy(table_ref.at[rest], table.at[rest], sems.at[4])
    keep = pltpu.make_async_copy(table.at[rest], out_ref.at[rest], sems.at[5])
    start_from(warm_ref, x_ref, p_ref)
    for load in loads:
        load.wait()
    fetch.start()

    def midway():
        fetch.wait()
        keep.start()

    conjugate(
        gram_ref[...] * gram_scale, turned, weighted, inside, x_ref, r_ref, p_ref, g_ref, midway
    )
    give(x_ref, table)
    first = pl.ds(0, batch)
    put = pltpu.make_async_copy(table.at[first], out_ref.at[first], sems.at[6])
    put.start()
    put.wait()
    keep.wait()


def solve_items(built, table, gram, gram_scale):
    blocks = built[2].shape[0]
    vmem = pl.BlockSpec(memory_space=pltpu.VMEM)
    hbm = pl.BlockSpec(memory_space=pltpu.HBM)
    return pl.pallas_call(
        functools.partial(solve_items_kernel, gram_scale),
        in_specs=[hbm] * 4 + [vmem, vmem, hbm],
        out_specs=hbm,
        out_shape=jax.ShapeDtypeStruct(table.shape, jnp.float32),
        scratch_shapes=[pltpu.VMEM(table.shape, jnp.float32)]
        + matrices(blocks)
        + [pltpu.SemaphoreType.DMA((7,))],
        compiler_params=pltpu.CompilerParams(vmem_limit_bytes=48 << 20),
        name="solve_items",
    )(*[hold(x) for x in built], table[: 4 * blocks], gram, hold(table))


def hold(values):
    return pltpu.with_memory_space_constraint(values, pltpu.HBM)


def exchange(values):
    return lax.all_to_all(values, AXES, split_axis=0, concat_axis=0, tiled=True)


def local_gram(table):
    return jnp.dot(
        table.T, table, precision=lax.Precision.HIGH, preferred_element_type=jnp.float32
    )


def shards(
    user_table,
    item_table,
    item_owner,
    item_row,
    user_confidence,
    user_rating,
    user_counts,
    user_owner,
    user_row,
    item_confidence,
    item_rating,
    item_counts,
):
    devices = lax.axis_size(AXES)
    tab_rows, width = user_table.shape
    blocks = user_counts.shape[0]
    batch = blocks * user_counts.shape[1]
    gram_scale = global_weight / (tab_rows * devices)

    def by_block(values):
        return values.reshape(blocks, -1)

    requests, item_slots, user_slots, places = bucket(
        by_block(item_owner),
        by_block(item_row),
        by_block(user_owner),
        by_block(user_row),
        item_table,
        batch,
    )
    came = exchange(requests[:, None, :])[:, 0]
    wanted = came[:, :width].astype(jnp.int32)
    gram_row = jnp.sum(came[:, width:], 0, keepdims=True)
    most = jnp.max(wanted[:, -1])
    fresh = jnp.minimum(wanted[:, PAD : 2 * PAD], batch - 1)

    replies = exchange(gather(0, CAP, PAD, wanted, item_table, gram_row))
    early = gather(PAD + PATCH, CAP - PATCH, EARLY, wanted, user_table)
    still = local_gram(user_table[batch:])
    early, still, replies = lax.optimization_barrier((early, still, replies))
    early = exchange(early)
    new_users, patch = solve_users(
        item_slots,
        wanted,
        user_counts,
        replies.reshape(-1, width),
        by_block(user_confidence),
        by_block(user_rating),
        user_table,
        still,
        gram_scale,
    )
    patch, early = lax.optimization_barrier((patch, early))
    patch = exchange(patch)

    def another(state):
        done, kept = state
        narrow = new_users[:batch].astype(jnp.bfloat16)
        rows = narrow[lax.dynamic_slice_in_dim(fresh, done, SLOT, 1)]
        return done + SLOT, lax.dynamic_update_slice(kept, exchange(rows), (0, done - PATCH, 0))

    _, more = lax.while_loop(lambda state: state[0] < most, another, (jnp.int32(PATCH), replies))
    rows = unsort(user_slots, early.reshape(-1, width))
    patch, rows = lax.optimization_barrier((patch, rows))
    gram_row = jnp.sum(patch[:, PATCH:].astype(jnp.float32), (0, 1))
    user_gram = exchange(jnp.broadcast_to(gram_row[None, None], (devices, 1, width)))[:, 0]
    built = build_items(
        places,
        item_counts,
        rows.reshape(-1, width),
        patch.reshape(-1, width),
        more,
        by_block(item_confidence),
        by_block(item_rating),
    )
    return (new_users, solve_items(built, item_table, user_gram, gram_scale))


def solution(mesh):
    spec = P(AXES, None)
    flat = P(AXES)
    in_specs = (spec, spec, spec, flat, flat, flat, spec, spec, flat, flat, flat, spec)
    return jax.shard_map(
        shards, mesh=mesh, in_specs=in_specs, out_specs=(spec, spec), check_vma=False
    )
```

```python
import functools

import jax
import jax.numpy as jnp
from jax import lax
from jax.experimental import pallas as pl
from jax.experimental.pallas import tpu as pltpu
from jax.sharding import PartitionSpec as P

ITERS = 8
AXES = ("gx", "gy")
LIVE = 112
PAD = 64
CAP = 60
PATCH = 14
SLOT = 16
EARLY = 48
TOGETHER = 4
STRIDE = 12
LANES = 128

ridge_weight = 1.0
global_weight = 256.0
guard_eps = 1e-06


def bucket_kernel(batch, *refs):
    inputs, (request_ref, slot0, slot1, place_ref) = refs[:5], refs[5:9]
    copies = [
        pltpu.make_async_copy(source, target, refs[14].at[k])
        for k, (source, target) in enumerate(zip(inputs, refs[9:14]))
    ]
    owner0, row0, owner1, row1, table_ref = refs[9:14]
    for copy in copies:
        copy.start()
    for copy in copies:
        copy.wait()

    chunks = owner0.shape[0]
    sub = lax.broadcasted_iota(jnp.int32, (LANES, LANES), 0)
    lane = lax.broadcasted_iota(jnp.int32, (LANES, LANES), 1)
    below = jnp.where(sub < lane, 1.0, 0.0)
    prefix = jnp.concatenate([below, jnp.ones_like(below)], 1).astype(jnp.bfloat16)
    place = sub % PAD
    first_half = sub < PAD
    group = 24
    zero = jnp.zeros((LANES, LANES), jnp.float32)
    wide = jnp.concatenate([zero, zero], 1)
    steps = chunks // group
    shares = [table_ref.shape[0] * part // (16 * steps) for part in (9, 6)]

    def add_gram(total, start, count):
        rows = table_ref[pl.ds(pl.multiple_of(start, LANES), count), :]
        head = rows.astype(jnp.bfloat16)
        rest = (rows - head.astype(jnp.float32)).astype(jnp.bfloat16)
        return total + jnp.dot(
            rows.T.astype(jnp.bfloat16),
            jnp.concatenate([head, rest], 1),
            preferred_element_type=jnp.float32,
        )

    def step(half, g, state):
        carry, wanted, gram = state
        gram = add_gram(gram, half * steps * shares[0] + g * shares[half], shares[half])
        start = pl.multiple_of(g * group, group)
        owners = (owner0, owner1)[half][pl.ds(start, group), :]
        rows = (row0, row1)[half][pl.ds(start, group), :]
        position = lax.broadcasted_iota(jnp.int32, owners.shape, 1)
        masked = jnp.where(position < LIVE, owners, -1)
        unit = jnp.where(rows < batch, 1.0, float(PAD)) if half == 1 else None
        hot = []
        counted = []
        for c in range(group):
            hit = sub == masked[c : c + 1, :]
            hot.append(jnp.where(hit, 1.0, 0.0))
            tally = hot[c] if half == 0 else jnp.where(hit, unit[c : c + 1, :], 0.0)
            counted.append(
                jnp.dot(tally.astype(jnp.bfloat16), prefix, preferred_element_type=jnp.float32)
            )
        ranks = []
        for c in range(group):
            before = counted[c][:, :LANES] + carry
            ranks.append(jnp.sum(before * hot[c], 0, keepdims=True).astype(jnp.int32))
            carry = carry + counted[c][:, LANES:]
        ranks = jnp.concatenate(ranks, 0)
        if half == 1:
            ranks = jnp.where(rows < batch, ranks % PAD, CAP - 1 - ranks // PAD)
        high = (rows // PAD).astype(jnp.float32)
        low = (rows % PAD).astype(jnp.float32)
        if half == 1:
            high, low = low, high
        lane_row = position.astype(jnp.float32)
        puts = []
        for c in range(group):
            chosen = place == ranks[c : c + 1, :]
            value = jnp.where(first_half, high[c : c + 1, :], low[c : c + 1, :])
            put = jnp.where(chosen, value, 0.0).astype(jnp.bfloat16)
            if half == 1:
                spot = jnp.where(
                    first_half, lane_row[c : c + 1, :], (g * group + c).astype(jnp.float32)
                )
                put = jnp.concatenate(
                    [put, jnp.where(chosen, spot, 0.0).astype(jnp.bfloat16)], 0
                )
            puts.append(put)
        wanted = wanted + lax.dot_general(
            jnp.concatenate(hot, 1).astype(jnp.bfloat16),
            jnp.concatenate(puts, 1),
            (((1,), (1,)), ((), ())),
            preferred_element_type=jnp.float32,
        )
        if half == 0:
            slot0[pl.ds(start, group), :] = owners * PAD + ranks
        else:
            slot1[pl.ds(start, group), :] = owners * EARLY + jnp.where(
                ranks < PATCH, EARLY - 1, ranks - PATCH
            )
        return carry, wanted, gram

    _, first, gram = lax.fori_loop(0, steps, functools.partial(step, 0), (zero, zero, wide))
    tally, second, gram = lax.fori_loop(0, steps, functools.partial(step, 1), (zero, wide, gram))
    done = steps * sum(shares)
    gram = add_gram(gram, done, table_ref.shape[0] - done)
    cross = gram[:, LANES:]
    spots = second[:, LANES:]
    second = second[:, :LANES]
    first = first * PAD + pltpu.roll(first, PAD, 1)
    second = second * PAD + pltpu.roll(second, PAD, 1)
    spots = spots + pltpu.roll(spots, PAD, 1) * LANES
    renewed = tally.astype(jnp.int32) % PAD
    most = jnp.max(renewed).astype(jnp.float32)
    request = jnp.where(lane < PAD, first, second)
    request_ref[:, :LANES] = jnp.where(lane == LANES - 1, most, request)
    request_ref[:, LANES:] = gram[:, :LANES] + cross + cross.T
    others = tally.astype(jnp.int32) // PAD
    used = (lane < renewed) | (lane >= CAP - others)
    places = jnp.where(used, spots.astype(jnp.int32), chunks * LANES)
    places = jnp.where(lane == PAD - 2, most.astype(jnp.int32), places)
    place_ref[...] = jnp.where(lane == PAD - 1, renewed, places)


def bucket(owner0, row0, owner1, row1, table, batch):
    slots = jax.ShapeDtypeStruct(owner0.shape, jnp.int32)
    inputs = (owner0, row0, owner1, row1, table)
    return pl.pallas_call(
        functools.partial(bucket_kernel, batch),
        in_specs=[pl.BlockSpec(memory_space=pltpu.HBM)] * 5,
        out_shape=(
            jax.ShapeDtypeStruct((LANES, 2 * LANES), jnp.float32),
            slots,
            slots,
            jax.ShapeDtypeStruct((LANES, LANES), jnp.int32),
        ),
        scratch_shapes=[pltpu.VMEM(x.shape, x.dtype) for x in inputs]
        + [pltpu.SemaphoreType.DMA((5,))],
        compiler_params=pltpu.CompilerParams(vmem_limit_bytes=32 << 20),
        name="bucket",
    )(*[hold(x) for x in inputs])


def gather_kernel(first, count, per_step, request_ref, table_ref, *refs):
    out_ref, wide = refs[-2:]
    base = pl.program_id(0) * per_step
    depth = wide.shape[1]
    last = jnp.zeros((depth - count, LANES), jnp.float32)
    if len(refs) == 3:
        row = refs[0][...]
        head = row.astype(jnp.bfloat16).astype(jnp.float32)
        last = jnp.concatenate([head, row - head, last[2:]], 0)
    for k in range(2):
        wide[k, count:, :] = last

    sub = lax.broadcasted_iota(jnp.int32, (8, LANES), 0)

    def one(s, state):
        buffer = wide.at[s % 2]
        for q in range(0, count, 8):
            part = None
            for i in range(min(8, count - q)):
                index = request_ref[base + s, first + q + i]
                row = jnp.broadcast_to(table_ref[pl.ds(index, 1), :], (8, LANES))
                part = row if part is None else jnp.where(sub == i, row, part)
            height = min(8, count - q)
            buffer[pl.ds(q, height), :] = part[:height]
        out_ref[s] = buffer[...].astype(jnp.bfloat16)
        return state

    lax.fori_loop(0, per_step, one, 0)


def gather(first, count, depth, requests, table, extra=None):
    devices = requests.shape[0]
    steps = 8
    per_step = devices // steps
    more = () if extra is None else (extra,)
    return pl.pallas_call(
        functools.partial(gather_kernel, first, count, per_step),
        grid=(steps,),
        in_specs=[
            pl.BlockSpec(memory_space=pltpu.SMEM),
            pl.BlockSpec(memory_space=pltpu.VMEM),
        ]
        + [pl.BlockSpec(extra.shape, lambda i: (0, 0)) for extra in more],
        out_specs=pl.BlockSpec((per_step, depth, LANES), lambda i: (i, 0, 0)),
        out_shape=pltpu.HBM((devices, depth, LANES), jnp.bfloat16),
        scratch_shapes=[pltpu.VMEM((2, depth, LANES), jnp.float32)],
        compiler_params=pltpu.CompilerParams(vmem_limit_bytes=32 << 20),
        name="gather_rows",
    )(requests, table, *more)


def unsort_kernel(slot_ref, reply_ref, out_ref, wide):
    widen(reply_ref, wide)

    def one(b, state):
        for t in range(LIVE):
            out_ref[b, pl.ds(t, 1), :] = wide[pl.ds(slot_ref[b, t], 1), :]
        out_ref[b, LIVE:, :] = jnp.zeros((LANES - LIVE, LANES), jnp.float32)
        return state

    lax.fori_loop(0, out_ref.shape[0], one, 0)


def unsort(slots, replies):
    blocks = slots.shape[0]
    return pl.pallas_call(
        unsort_kernel,
        in_specs=[pl.BlockSpec(memory_space=pltpu.SMEM), pl.BlockSpec(memory_space=pltpu.VMEM)],
        out_specs=pl.BlockSpec(memory_space=pltpu.VMEM),
        out_shape=pltpu.HBM((blocks, LANES, LANES), jnp.float32),
        scratch_shapes=[pltpu.VMEM(replies.shape, jnp.float32)],
        compiler_params=pltpu.CompilerParams(vmem_limit_bytes=32 << 20),
        name="unsort_rows",
    )(slots, replies)


def fold(value):
    return value + pltpu.roll(value, 4, 0)


def split(value):
    top = lax.broadcasted_iota(jnp.int32, value.shape, 0) < 4
    head = value.astype(jnp.bfloat16).astype(jnp.float32)
    return jnp.where(top, head, value - head).astype(jnp.bfloat16)


def widen(source, target):
    step = 512

    def one(i, state):
        start = pl.multiple_of(i * step, step)
        target[pl.ds(start, step), :] = source[pl.ds(start, step), :].astype(jnp.float32)
        return state

    lax.fori_loop(0, source.shape[0] // step, one, 0)


def spread_weights(conf_ref, weight_wide):
    blocks = conf_ref.shape[0]
    conf_turned = jnp.concatenate(
        [conf_ref[...], jnp.zeros((LANES - blocks, LANES), jnp.float32)], 0
    ).T
    for b in range(blocks):
        weight_wide[b] = jnp.broadcast_to(conf_turned[:, b : b + 1], (LANES, LANES))


def build_blocks(
    first, rows, count_ref, conf_ref, rating_ref, weight_wide, turned, weighted, inside, right, base=None
):
    base = first if base is None else base
    sub = lax.broadcasted_iota(jnp.int32, (8, LANES), 0)
    lane = lax.broadcasted_iota(jnp.int32, (8, LANES), 1)
    which = sub % 4
    sums = []
    for c, fetched in enumerate(rows):
        b = first + c
        pair, side = base // 2 + c // 2, pl.ds(c % 2 * LANES, LANES)
        turned[pair, :, side] = fetched.astype(jnp.bfloat16).T
        weighted[pair, side, :] = (weight_wide[b] * fetched).astype(jnp.bfloat16)
        end0 = count_ref[b, 0]
        end1 = end0 + count_ref[b, 1]
        end2 = end1 + count_ref[b, 2]
        end3 = end2 + count_ref[b, 3]
        begin = jnp.where(which < 2, jnp.where(which == 0, 0, end0), jnp.where(which == 2, end1, end2))
        end = jnp.where(which < 2, jnp.where(which == 0, end0, end1), jnp.where(which == 2, end2, end3))
        mask = jnp.where((lane >= begin) & (lane < end), 1.0, 0.0)
        inside[base + c] = mask
        target = conf_ref[pl.ds(b, 1), :] * rating_ref[pl.ds(b, 1), :] * mask
        sums.append(
            jnp.dot(split(target), fetched.astype(jnp.bfloat16), preferred_element_type=jnp.float32)
        )
    for c, part in enumerate(sums):
        right[base + c] = fold(part)


def start_from(warm_ref, x_ref, p_ref):
    for b in range(x_ref.shape[0]):
        warm = warm_ref[pl.ds(4 * b, 4), :]
        both = jnp.concatenate([warm, warm], 0)
        x_ref[b] = both
        p_ref[b] = both


def give(x_ref, out_ref):
    for b in range(x_ref.shape[0]):
        out_ref[pl.ds(4 * b, 4), :] = x_ref[b, :4, :]


def local_images(cut, turned, weighted, inside, ids):
    nought = jnp.zeros((8, LANES), jnp.bfloat16)
    along = []
    for c in range(0, len(ids), 2):
        out = jnp.dot(
            jnp.concatenate(cut[c : c + 2], 0),
            turned[ids[c] // 2],
            preferred_element_type=jnp.float32,
        )
        along += [fold(out[:8, :LANES]), fold(out[8:, LANES:])]
    back = []
    for c in range(0, len(ids), 2):
        one, two = [split(along[k] * inside[ids[k]]) for k in (c, c + 1)]
        both = jnp.concatenate(
            [jnp.concatenate([one, nought], 1), jnp.concatenate([nought, two], 1)], 0
        )
        out = jnp.dot(both, weighted[ids[c] // 2], preferred_element_type=jnp.float32)
        back += [out[:8], out[8:]]
    return back


def conjugate(gram, turned, weighted, inside, x_ref, r_ref, p_ref, g_ref, midway=None):
    blocks = x_ref.shape[0]
    gram_head = gram.astype(jnp.bfloat16)
    gram_tail = (gram - gram_head.astype(jnp.float32)).astype(jnp.bfloat16)
    gram_both = jnp.concatenate([gram_head, gram_tail], 1)
    group = 24

    def apply_system(g):
        ids = [g * group + c for c in range(group)]
        dirs = [p_ref[b] for b in ids]
        cut = [split(d) for d in dirs]
        shared = jnp.dot(jnp.concatenate(cut, 0), gram_both, preferred_element_type=jnp.float32)
        back = local_images(cut, turned, weighted, inside, ids)
        images = []
        for c in range(group):
            part = shared[8 * c : 8 * c + 8]
            images.append(
                fold(back[c] + part[:, :LANES] + part[:, LANES:]) + ridge_weight * dirs[c]
            )
        return ids, dirs, images

    for g in range(blocks // group):
        if midway is None:
            ids, _, images = apply_system(g)
        else:
            ids = [g * group + c for c in range(group)]
            shared = jnp.dot(
                jnp.concatenate([split(p_ref[b]) for b in ids], 0),
                gram_both,
                preferred_element_type=jnp.float32,
            )
            shared = shared[:, :LANES] + shared[:, LANES:]
            images = [fold(shared[8 * c : 8 * c + 8]) for c in range(group)]
        for c in range(group):
            resid = r_ref[ids[c]] - images[c]
            r_ref[ids[c]] = resid
            p_ref[ids[c]] = resid
            g_ref[ids[c]] = jnp.broadcast_to(
                jnp.sum(resid * resid, -1, keepdims=True), (8, LANES)
            )

    def iterate(i, state):
        for g in range(blocks // group):
            ids, dirs, images = apply_system(g)
            for c in range(group):
                b = ids[c]
                norm_now = g_ref[b]
                step_size = norm_now / (
                    jnp.sum(dirs[c] * images[c], -1, keepdims=True) + guard_eps
                )
                x_ref[b] = x_ref[b] + step_size * dirs[c]
                resid = r_ref[b] - step_size * images[c]
                r_ref[b] = resid
                norm_next = jnp.sum(resid * resid, -1, keepdims=True)
                p_ref[b] = resid + norm_next / (norm_now + guard_eps) * dirs[c]
                g_ref[b] = jnp.broadcast_to(norm_next, (8, LANES))
        return state

    lax.fori_loop(0, ITERS // 2, iterate, 0)
    if midway is not None:
        midway()
    lax.fori_loop(ITERS // 2, ITERS, iterate, 0)


def solve_users_kernel(
    gram_scale,
    slot_ref,
    wanted_ref,
    count_ref,
    reply_ref,
    conf_ref,
    rating_ref,
    table_ref,
    still_ref,
    out_ref,
    patch_ref,
    narrow,
    wide,
    table,
    weight_wide,
    rows,
    turned,
    weighted,
    inside,
    x_ref,
    r_ref,
    p_ref,
    g_ref,
    sems,
):
    blocks = conf_ref.shape[0]
    batch = 4 * blocks
    parts = 4
    depth = reply_ref.shape[0] // parts
    fetches = []
    for k in range(parts):
        part = pl.ds(k * depth, depth)
        fetches.append(pltpu.make_async_copy(reply_ref.at[part], narrow.at[part], sems.at[k]))
        fetches[k].start()
    load = pltpu.make_async_copy(table_ref, table, sems.at[parts])
    load.start()
    rest = pl.ds(batch, table_ref.shape[0] - batch)
    keep = pltpu.make_async_copy(table.at[rest], out_ref.at[rest], sems.at[parts + 1])
    spread_weights(conf_ref, weight_wide)
    rows[...] = jnp.zeros_like(rows)
    for k in range(parts):
        part = pl.ds(k * depth, depth)
        fetches[k].wait()
        widen(narrow.at[part], wide.at[part])

    def build(g, state):
        first = g * TOGETHER
        for c in range(TOGETHER):
            for t in range(LIVE):
                rows[c, pl.ds(t, 1), :] = wide[pl.ds(slot_ref[first + c, t], 1), :]
        build_blocks(
            first,
            [rows[c] for c in range(TOGETHER)],
            count_ref,
            conf_ref,
            rating_ref,
            weight_wide,
            turned,
            weighted,
            inside,
            r_ref,
        )
        return state

    lax.fori_loop(0, blocks // TOGETHER, build, 0)
    load.wait()
    keep.start()
    start_from(table, x_ref, p_ref)
    gram = wide[pl.ds(CAP, LANES, stride=PAD), :] + wide[pl.ds(CAP + 1, LANES, stride=PAD), :]
    conjugate(gram * gram_scale, turned, weighted, inside, x_ref, r_ref, p_ref, g_ref)
    give(x_ref, table)
    put = pltpu.make_async_copy(
        table.at[pl.ds(0, batch)], out_ref.at[pl.ds(0, batch)], sems.at[parts + 2]
    )
    put.start()

    solved = table[pl.ds(0, batch), :]
    head = solved.astype(jnp.bfloat16)
    rest = (solved - head.astype(jnp.float32)).astype(jnp.bfloat16)
    head_turned = head.astype(jnp.float32).T.astype(jnp.bfloat16)
    cross = jnp.dot(head_turned, rest, preferred_element_type=jnp.float32)
    gram = jnp.dot(head_turned, head, preferred_element_type=jnp.float32) + cross + cross.T
    rows[0] = still_ref[...] + gram

    def one(o, state):
        buffer = rows.at[1, pl.ds(pl.multiple_of(o % 2 * SLOT, SLOT), SLOT)]
        for i in range(PATCH):
            buffer[pl.ds(i, 1), :] = table[pl.ds(wanted_ref[o, PAD + i], 1), :]
        share = rows[0, pl.ds(o, 1), :]
        top = share.astype(jnp.bfloat16).astype(jnp.float32)
        buffer[pl.ds(PATCH, 1), :] = top
        buffer[pl.ds(PATCH + 1, 1), :] = share - top
        patch_ref[o] = buffer[...].astype(jnp.bfloat16)
        return state

    lax.fori_loop(0, wanted_ref.shape[0], one, 0)
    put.wait()
    keep.wait()


def solve_users(slots, wanted, counts, replies, confidence, rating, table, still, gram_scale):
    blocks = confidence.shape[0]
    vmem = pl.BlockSpec(memory_space=pltpu.VMEM)
    smem = pl.BlockSpec(memory_space=pltpu.SMEM)
    hbm = pl.BlockSpec(memory_space=pltpu.HBM)
    return pl.pallas_call(
        functools.partial(solve_users_kernel, gram_scale),
        in_specs=[smem, smem, smem, hbm, vmem, vmem, hbm, vmem],
        out_specs=[hbm, vmem],
        out_shape=[
            jax.ShapeDtypeStruct(table.shape, jnp.float32),
            pltpu.HBM((wanted.shape[0], SLOT, LANES), jnp.bfloat16),
        ],
        scratch_shapes=[
            pltpu.VMEM(replies.shape, jnp.bfloat16),
            pltpu.VMEM(replies.shape, jnp.float32),
            pltpu.VMEM(table.shape, jnp.float32),
            pltpu.VMEM((blocks, LANES, LANES), jnp.float32),
            pltpu.VMEM((TOGETHER, LANES, LANES), jnp.float32),
        ]
        + matrices(blocks)
        + [pltpu.SemaphoreType.DMA((7,))],
        compiler_params=pltpu.CompilerParams(vmem_limit_bytes=48 << 20),
        name="solve_users",
    )(slots, wanted, counts, hold(replies), confidence, rating, hold(table), still)


def matrices(blocks):
    return [
        pltpu.VMEM((blocks // 2, LANES, 2 * LANES), jnp.bfloat16),
        pltpu.VMEM((blocks // 2, 2 * LANES, LANES), jnp.bfloat16),
    ] + [pltpu.VMEM((blocks, 8, LANES), jnp.float32)] * 5


def build_items_kernel(
    place_ref,
    count_ref,
    rows_ref,
    patch_ref,
    more_ref,
    conf_ref,
    rating_ref,
    warm_ref,
    turned,
    weighted,
    inside,
    right,
    wide,
    more_narrow,
    more_wide,
    weight_wide,
    rows,
    sem,
):
    def renew(o, state):
        for k in range(PATCH):
            rows[pl.ds(place_ref[o, k], 1), :] = wide[pl.ds(o * SLOT + k, 1), :]
        return state

    def renew_more(o, state):
        count = place_ref[o, PAD - 1]

        @pl.when(count > PATCH)
        def _():
            pltpu.sync_copy(more_ref.at[o], more_narrow)
            more_wide[...] = more_narrow[...].astype(jnp.float32)

            def put(k, inner):
                rows[pl.ds(place_ref[o, k], 1), :] = more_wide[pl.ds(k - PATCH, 1), :]
                return inner

            lax.fori_loop(PATCH, count, put, 0)

        return state

    @pl.when(pl.program_id(0) == 0)
    def _():
        load = pltpu.make_async_copy(rows_ref, rows.at[pl.ds(0, rows_ref.shape[0])], sem)
        load.start()
        widen(patch_ref, wide)
        spread_weights(conf_ref, weight_wide)
        load.wait()
        lax.fori_loop(0, place_ref.shape[0], renew, 0, unroll=4)

        @pl.when(place_ref[0, PAD - 2] > PATCH)
        def _():
            lax.fori_loop(0, place_ref.shape[0], renew_more, 0)

    first = pl.program_id(0) * STRIDE
    start = pl.multiple_of(first * LANES, LANES)
    build_blocks(
        first,
        [rows[pl.ds(start + c * LANES, LANES), :] for c in range(STRIDE)],
        count_ref,
        conf_ref,
        rating_ref,
        weight_wide,
        turned,
        weighted,
        inside,
        right,
        0,
    )
    warm = warm_ref[pl.ds(pl.multiple_of(first * 4, 8), 4 * STRIDE), :]
    ids = list(range(STRIDE))
    begin = [jnp.concatenate([warm[4 * c : 4 * c + 4]] * 2, 0) for c in ids]
    back = local_images([split(x) for x in begin], turned, weighted, inside, ids)
    for c in ids:
        right[c] = right[c] - fold(back[c]) - ridge_weight * begin[c]


def build_items(places, counts, rows, patch, more, confidence, rating, warm):
    blocks = confidence.shape[0]
    vmem = pl.BlockSpec(memory_space=pltpu.VMEM)
    smem = pl.BlockSpec(memory_space=pltpu.SMEM)
    hbm = pl.BlockSpec(memory_space=pltpu.HBM)
    pairs = STRIDE // 2
    shapes = [
        ((blocks // 2, LANES, 2 * LANES), jnp.bfloat16, pairs),
        ((blocks // 2, 2 * LANES, LANES), jnp.bfloat16, pairs),
        ((blocks, 8, LANES), jnp.float32, STRIDE),
        ((blocks, 8, LANES), jnp.float32, STRIDE),
    ]
    return pl.pallas_call(
        build_items_kernel,
        grid=(blocks // STRIDE,),
        in_specs=[smem, smem, hbm, vmem, hbm, vmem, vmem, vmem],
        out_specs=[
            pl.BlockSpec((step,) + shape[1:], lambda i: (i, 0, 0)) for shape, _, step in shapes
        ],
        out_shape=[pltpu.HBM(shape, kind) for shape, kind, _ in shapes],
        scratch_shapes=[
            pltpu.VMEM(patch.shape, jnp.float32),
            pltpu.VMEM(more.shape[1:], jnp.bfloat16),
            pltpu.VMEM(more.shape[1:], jnp.float32),
            pltpu.VMEM((blocks, LANES, LANES), jnp.float32),
            pltpu.VMEM((blocks * LANES + 8, LANES), jnp.float32),
            pltpu.SemaphoreType.DMA,
        ],
        compiler_params=pltpu.CompilerParams(vmem_limit_bytes=48 << 20),
        name="build_items",
    )(places, counts, hold(rows), patch, hold(more), confidence, rating, warm)


def solve_items_kernel(gram_scale, *refs):
    built, (warm_ref, gram_ref, table_ref, out_ref, table) = refs[:4], refs[4:9]
    turned, weighted, inside, x_ref, r_ref, p_ref, g_ref, sems = refs[9:]
    loads = [
        pltpu.make_async_copy(source, target, sems.at[k])
        for k, (source, target) in enumerate(zip(built, (turned, weighted, inside, r_ref)))
    ]
    for load in loads:
        load.start()
    batch = 4 * x_ref.shape[0]
    rest = pl.ds(batch, table.shape[0] - batch)
    fetch = pltpu.make_async_copy(table_ref.at[rest], table.at[rest], sems.at[4])
    keep = pltpu.make_async_copy(table.at[rest], out_ref.at[rest], sems.at[5])
    start_from(warm_ref, x_ref, p_ref)
    for load in loads:
        load.wait()
    fetch.start()

    def midway():
        fetch.wait()
        keep.start()

    conjugate(
        gram_ref[...] * gram_scale, turned, weighted, inside, x_ref, r_ref, p_ref, g_ref, midway
    )
    give(x_ref, table)
    first = pl.ds(0, batch)
    put = pltpu.make_async_copy(table.at[first], out_ref.at[first], sems.at[6])
    put.start()
    put.wait()
    keep.wait()


def solve_items(built, table, gram, gram_scale):
    blocks = built[2].shape[0]
    vmem = pl.BlockSpec(memory_space=pltpu.VMEM)
    hbm = pl.BlockSpec(memory_space=pltpu.HBM)
    return pl.pallas_call(
        functools.partial(solve_items_kernel, gram_scale),
        in_specs=[hbm] * 4 + [vmem, vmem, hbm],
        out_specs=hbm,
        out_shape=jax.ShapeDtypeStruct(table.shape, jnp.float32),
        scratch_shapes=[pltpu.VMEM(table.shape, jnp.float32)]
        + matrices(blocks)
        + [pltpu.SemaphoreType.DMA((7,))],
        compiler_params=pltpu.CompilerParams(vmem_limit_bytes=48 << 20),
        name="solve_items",
    )(*[hold(x) for x in built], table[: 4 * blocks], gram, hold(table))


def hold(values):
    return pltpu.with_memory_space_constraint(values, pltpu.HBM)


def exchange(values):
    return lax.all_to_all(values, AXES, split_axis=0, concat_axis=0, tiled=True)


def local_gram(table):
    return jnp.dot(
        table.T, table, precision=lax.Precision.HIGH, preferred_element_type=jnp.float32
    )


def shards(
    user_table,
    item_table,
    item_owner,
    item_row,
    user_confidence,
    user_rating,
    user_counts,
    user_owner,
    user_row,
    item_confidence,
    item_rating,
    item_counts,
):
    devices = lax.axis_size(AXES)
    tab_rows, width = user_table.shape
    blocks = user_counts.shape[0]
    batch = blocks * user_counts.shape[1]
    gram_scale = global_weight / (tab_rows * devices)

    def by_block(values):
        return values.reshape(blocks, -1)

    requests, item_slots, user_slots, places = bucket(
        by_block(item_owner),
        by_block(item_row),
        by_block(user_owner),
        by_block(user_row),
        item_table,
        batch,
    )
    came = exchange(requests[:, None, :])[:, 0]
    wanted = came[:, :width].astype(jnp.int32)
    gram_row = jnp.sum(came[:, width:], 0, keepdims=True)
    most = jnp.max(wanted[:, -1])
    fresh = jnp.minimum(wanted[:, PAD : 2 * PAD], batch - 1)

    replies = exchange(gather(0, CAP, PAD, wanted, item_table, gram_row))
    early = gather(PAD + PATCH, CAP - PATCH, EARLY, wanted, user_table)
    still = local_gram(user_table[batch:])
    early, still, replies = lax.optimization_barrier((early, still, replies))
    early = exchange(early)
    new_users, patch = solve_users(
        item_slots,
        wanted,
        user_counts,
        replies.reshape(-1, width),
        by_block(user_confidence),
        by_block(user_rating),
        user_table,
        still,
        gram_scale,
    )
    patch, early = lax.optimization_barrier((patch, early))
    patch = exchange(patch)

    def another(state):
        done, kept = state
        narrow = new_users[:batch].astype(jnp.bfloat16)
        rows = narrow[lax.dynamic_slice_in_dim(fresh, done, SLOT, 1)]
        return done + SLOT, lax.dynamic_update_slice(kept, exchange(rows), (0, done - PATCH, 0))

    _, more = lax.while_loop(lambda state: state[0] < most, another, (jnp.int32(PATCH), replies))
    rows = unsort(user_slots, early.reshape(-1, width))
    patch, rows = lax.optimization_barrier((patch, rows))
    gram_row = jnp.sum(patch[:, PATCH:].astype(jnp.float32), (0, 1))
    user_gram = exchange(jnp.broadcast_to(gram_row[None, None], (devices, 1, width)))[:, 0]
    built = build_items(
        places,
        item_counts,
        rows.reshape(-1, width),
        patch.reshape(-1, width),
        more,
        by_block(item_confidence),
        by_block(item_rating),
        item_table[:batch],
    )
    return (new_users, solve_items(built, item_table, user_gram, gram_scale))


def solution(mesh):
    spec = P(AXES, None)
    flat = P(AXES)
    in_specs = (spec, spec, spec, flat, flat, flat, spec, spec, flat, flat, flat, spec)
    return jax.shard_map(
        shards, mesh=mesh, in_specs=in_specs, out_specs=(spec, spec), check_vma=False
    )
```
